32 devices in a mesh: row: 8 (over y, x, core), col: 4 (over z).
Axes of the slice: x: 2, y: 2, z: 4, core: 2. Of those that a mesh axis runs over, the one named last changes fastest.
Arguments:
- latents: bfloat16 [512, 6144], P('col', 'row'), may hold values from -6 to 6
- w_in: bfloat16 [6144, 24576], P('row', 'col'), may hold values from -0.078125 to 0.078125
- w_out: bfloat16 [24576, 6144], P('col', 'row'), may hold values from -0.0390625 to 0.0390625
- cotangent: bfloat16 [512, 6144], P('col', 'row'), may hold values from -0.625 to 0.625
Outputs:
- mixed: bfloat16 [512, 6144], P('col', 'row')
- grad_w_in: bfloat16 [6144, 24576], P('row', 'col')
- grad_w_out: bfloat16 [24576, 6144], P('col', 'row')
The draws below stay inside these ranges and needn't reach their ends.
All inputs are finite; a program needn't handle non-finite values.
Results may differ from the reference program's by a relative error of at most 0.03.
Values may be sent and summed in bfloat16 or wider, within the bound.
No kernel may reach another device: no remote copies, remote signals or barrier semaphores. Data moves between devices by JAX's collectives and lax.ppermute only.
A program may use at most 128 MiB of HBM per device.

```python
import jax
import jax.numpy as jnp
from jax import lax

D = 6144
H = 24576
TOKENS = 512
N_ROW = 8
N_COL = 4


def steps_of(stream_key, dims, shards, least, high):
    level, own = 1.0, jax.random.fold_in(stream_key, 6)
    for position, blocks in shards:
        heights = jnp.exp(jax.random.uniform(jax.random.fold_in(own, position), (blocks,), jnp.float32, least / len(shards), high / len(shards)))
        level = level * jnp.repeat(heights, dims[position] // blocks).reshape([-1 if axis == position else 1 for axis in range(len(dims))])
    return level


def gaussian(rng, extent, width, reach, shards=(), dtype=jnp.bfloat16):
    level = steps_of(rng, extent, shards, -0.22, 0.18) if shards else 1.0
    drawn = jax.random.normal(rng, extent, jnp.float32) * width * level
    return jnp.minimum(jnp.maximum(drawn, -reach), reach).astype(dtype)


def setup_inputs(seed: int = 0) -> dict:
    keys = jax.random.split(jax.random.key(seed), 5)
    latents = gaussian(keys[0], (TOKENS, D), 1.0, 6.0, ((0, 4), (1, 8)))
    w_in = gaussian(keys[1], (D, H), D ** -0.5, 0.078125, ((0, 8), (1, 4)))
    w_out = gaussian(keys[2], (H, D), H ** -0.5, 0.0390625, ((0, 4), (1, 8)))
    cotangent = gaussian(keys[3], (TOKENS, D), (TOKENS ** -0.5), 0.625, ((0, 4), (1, 8)))
    return dict(latents=latents, w_in=w_in, w_out=w_out, cotangent=cotangent)


def gelu_parts(hidden):
    cdf = 0.5 * (1.0 + jax.scipy.special.erf(hidden * 0.7071067811865476))
    pdf = jnp.exp(-0.5 * hidden * hidden) * 0.3989422804014327
    return hidden * cdf, cdf + hidden * pdf


def reference(latents, w_in, w_out, cotangent):
    width_block = D // N_ROW
    hidden_block = H // N_COL

    def hidden_step(index, total):
        start = (index * width_block).astype(jnp.int32)
        feature_part = lax.dynamic_slice_in_dim(latents, start, width_block, 1)
        weight_part = lax.dynamic_slice_in_dim(w_in, start, width_block, 0)
        term = jnp.dot(feature_part, weight_part, preferred_element_type=jnp.float32)
        rounded = lax.optimization_barrier(term.astype(jnp.bfloat16))
        return total + rounded.astype(jnp.float32)

    hidden = lax.fori_loop(0, N_ROW, hidden_step, jnp.zeros((TOKENS, H), jnp.float32))
    act, slope = gelu_parts(hidden)
    act = act.astype(jnp.bfloat16)

    def mixed_step(index, total):
        start = (index * hidden_block).astype(jnp.int32)
        act_part = lax.dynamic_slice_in_dim(act, start, hidden_block, 1)
        weight_part = lax.dynamic_slice_in_dim(w_out, start, hidden_block, 0)
        term = jnp.dot(act_part, weight_part, preferred_element_type=jnp.float32)
        rounded = lax.optimization_barrier(term.astype(jnp.bfloat16))
        return total + rounded.astype(jnp.float32)

    mixed = lax.fori_loop(0, N_COL, mixed_step, jnp.zeros((TOKENS, D), jnp.float32)).astype(jnp.bfloat16)

    def act_step(index, total):
        start = (index * width_block).astype(jnp.int32)
        grad_part = lax.dynamic_slice_in_dim(cotangent, start, width_block, 1)
        weight_part = lax.dynamic_slice_in_dim(w_out, start, width_block, 1)
        term = lax.dot_general(grad_part, weight_part, (((1,), (1,)), ((), ())), preferred_element_type=jnp.float32)
        rounded = lax.optimization_barrier(term.astype(jnp.bfloat16))
        return total + rounded.astype(jnp.float32)

    grad_act = lax.fori_loop(0, N_ROW, act_step, jnp.zeros((TOKENS, H), jnp.float32))
    grad_hidden = (grad_act * slope).astype(jnp.bfloat16)
    grad_w_out = lax.dot_general(act, cotangent, (((0,), (0,)), ((), ())), preferred_element_type=jnp.float32).astype(jnp.bfloat16)
    grad_w_in = lax.dot_general(latents, grad_hidden, (((0,), (0,)), ((), ())), preferred_element_type=jnp.float32).astype(jnp.bfloat16)
    return mixed, grad_w_in, grad_w_out
```

```python
import jax
import jax.numpy as jnp
from jax import lax
from jax.sharding import PartitionSpec as P

f32 = jnp.float32
bf16 = jnp.bfloat16


def gelu_parts(hidden):
    cdf = 0.5 * (1.0 + jax.scipy.special.erf(hidden * 0.7071067811865476))
    pdf = jnp.exp(-0.5 * hidden * hidden) * 0.3989422804014327
    return (hidden * cdf, cdf + hidden * pdf)


def half(v, axis, index):
    return lax.slice_in_dim(v, index, index + 1, axis=axis)


def make(n_row, n_col):
    row_bits = n_row.bit_length() - 1
    col_bits = n_col.bit_length() - 1

    def swap(v, name, n, bit):
        return lax.ppermute(v, name, [(i, i ^ (1 << bit)) for i in range(n)])

    def relative(v):
        me = lax.axis_index("row")
        shape = v.shape
        v = v.reshape((2,) * row_bits + (shape[0] // n_row, shape[1]))
        for bit in range(row_bits):
            v = jnp.where((me >> bit) & 1 == 1, jnp.flip(v, bit), v)
        return v

    def scatter(v, order):
        for step, bit in enumerate(order):
            got = swap(half(v, bit, 1), "row", n_row, bit)
            v = half(v, bit, 0).astype(f32) + got.astype(f32)
            if step + 1 < len(order):
                v = v.astype(bf16)
        return v

    def gather(v, order):
        for bit in reversed(order):
            v = lax.concatenate([v, swap(v, "row", n_row, bit)], bit)
        return v

    def per_device(latents, w_in, w_out, cotangent):
        tokens, width = latents.shape
        hidden_width = w_in.shape[1]
        cut = hidden_width // 2
        forward = tuple(range(row_bits))
        orders = (forward, forward[:1] + forward[:0:-1])

        def spread(v):
            v = relative(v)[..., None, :, :]
            chunks = [v]
            whole = v
            for bit in range(col_bits):
                got = swap(whole, "col", n_col, bit)
                chunks.append(got)
                whole = lax.concatenate([whole, got], row_bits)
            return chunks

        xs = spread(latents)
        cs = spread(cotangent)
        flat = lambda v: v.reshape(-1, v.shape[-1])

        acts, grads = [], []
        for x, c in zip(xs, cs):
            lead = x.shape[:-1]
            act_parts, grad_parts = [], []
            for part, order in enumerate(orders):
                lo = part * cut
                hid = jnp.dot(flat(x), w_in[:, lo : lo + cut], preferred_element_type=f32)
                hid = scatter(hid.astype(bf16).reshape(lead + (cut,)), order)
                act, slope = gelu_parts(hid)
                act_parts.append(gather(act.astype(bf16), order))
                grad = lax.dot_general(
                    flat(c), w_out[lo : lo + cut], (((1,), (1,)), ((), ())), preferred_element_type=f32
                )
                grad = scatter(grad.astype(bf16).reshape(lead + (cut,)), order)
                grad_parts.append(gather((grad * slope).astype(bf16), order))
            acts.append(jnp.concatenate([flat(v) for v in act_parts], 1))
            grads.append(jnp.concatenate([flat(v) for v in grad_parts], 1))

        x_all = jnp.concatenate([flat(v) for v in xs], 0)
        c_all = jnp.concatenate([flat(v) for v in cs], 0)
        act_all = jnp.concatenate(acts, 0)
        grad_all = jnp.concatenate(grads, 0)

        mixed = jnp.dot(act_all, w_out, preferred_element_type=f32).astype(bf16)
        parts, at = [], 0
        for x in xs:
            rows = flat(x).shape[0]
            parts.append(mixed[at : at + rows].reshape(x.shape))
            at += rows
        for bit in reversed(range(col_bits)):
            got = swap(parts.pop(), "col", n_col, bit)
            at = 0
            for i, v in enumerate(parts):
                blocks = v.shape[row_bits]
                piece = lax.slice_in_dim(got, at, at + blocks, axis=row_bits)
                parts[i] = (v.astype(f32) + piece.astype(f32)).astype(bf16)
                at += blocks
        mixed = relative(parts[0].reshape(tokens, width)).reshape(tokens, width)

        grad_w_out = lax.dot_general(
            act_all, c_all, (((0,), (0,)), ((), ())), preferred_element_type=f32
        )
        x_t = lax.optimization_barrier(x_all.T)
        grad_w_in = jnp.dot(x_t, grad_all, preferred_element_type=f32)
        return (mixed, grad_w_in.astype(bf16), grad_w_out.astype(bf16))

    return per_device


def solution(mesh):
    placed = (P("col", "row"), P("row", "col"), P("col", "row"), P("col", "row"))
    return jax.shard_map(
        make(mesh.shape["row"], mesh.shape["col"]),
        mesh=mesh,
        in_specs=placed,
        out_specs=(P("col", "row"), P("row", "col"), P("col", "row")),
        check_vma=False,
    )
```

```python
import jax
import jax.numpy as jnp
from jax import lax
from jax.sharding import PartitionSpec as P

f32 = jnp.float32
bf16 = jnp.bfloat16


def gelu_parts(hidden):
    cdf = 0.5 * (1.0 + jax.scipy.special.erf(hidden * 0.7071067811865476))
    pdf = jnp.exp(-0.5 * hidden * hidden) * 0.3989422804014327
    return (hidden * cdf, cdf + hidden * pdf)


def make(n_row, n_col):
    row_bits = n_row.bit_length() - 1
    col_bits = n_col.bit_length() - 1
    first = tuple(range(1, row_bits))
    orders = (first, first[::-1])
    steps = len(first)

    def swap_core(v):
        return lax.ppermute(v, "row", [(i, i ^ 1) for i in range(n_row)])

    def swap_chip(v, step):
        return lax.ppermute(v, "row", [(i, i ^ (1 << orders[i & 1][step])) for i in range(n_row)])

    def swap_col(v, bit):
        return lax.ppermute(v, "col", [(i, i ^ (1 << bit)) for i in range(n_col)])

    def part(v, axis, index):
        return lax.slice_in_dim(v, index, index + 1, axis=axis)

    def flips(v, order, axis):
        me = lax.axis_index("row")
        for k, bit in enumerate(order):
            v = jnp.where((me >> bit) & 1 == 1, jnp.flip(v, axis + k), v)
        return v

    def relative(v):
        v = v.reshape((2,) * steps + (1, v.shape[0] >> steps, v.shape[1]))
        return flips(v, first, 0)

    def turn(v):
        return v.transpose(tuple(range(steps))[::-1] + tuple(range(steps, v.ndim)))

    def after(v, *tokens):
        return lax.optimization_barrier((v,) + tokens)[0]

    def flat(v):
        return v.reshape(-1, v.shape[-1])

    def scatter(parts):
        core = lax.axis_index("row") & 1
        second = turn(parts[1])
        got = swap_core(jnp.where(core == 0, second, parts[0]))
        v = jnp.where(core == 0, parts[0], second)
        v = (v.astype(f32) + got.astype(f32)).astype(bf16)
        seen = [v]
        for k in range(steps):
            got = swap_chip(part(v, k, 1), k)
            seen.append(got)
            v = part(v, k, 0).astype(f32) + got.astype(f32)
            if k + 1 < steps:
                v = v.astype(bf16)
        return v, seen

    def gather_chips(v, stop):
        for k in reversed(range(stop, steps)):
            v = lax.concatenate([v, swap_chip(v, k)], k)
        return v

    def per_device(latents, w_in, w_out, cotangent):
        tokens, width = latents.shape
        cut = w_in.shape[1] // 2
        core = lax.axis_index("row") & 1

        def double(v, bit):
            got = swap_col(v, bit)
            return got, lax.concatenate([v, got], steps)

        halves = [slice(h * cut, (h + 1) * cut) for h in (0, 1)]

        def up(x):
            parts = [jnp.dot(flat(x), w_in[:, h], preferred_element_type=f32) for h in halves]
            return scatter([v.astype(bf16).reshape(x.shape[:-1] + (cut,)) for v in parts])

        def back(c):
            parts = [
                lax.dot_general(flat(c), w_out[h], (((1,), (1,)), ((), ())), preferred_element_type=f32)
                for h in halves
            ]
            return scatter([v.astype(bf16).reshape(c.shape[:-1] + (cut,)) for v in parts])

        _, x_all = double(relative(latents), 0)
        _, c_all = double(relative(cotangent), 0)
        hid, seen_hid = up(x_all)
        grad, seen_grad = back(c_all)
        hids, grads = [hid], [grad]
        for bit in range(1, col_bits):
            x, x_all = double(x_all, bit)
            x = after(x, seen_hid[1], seen_grad[0])
            c, c_all = double(after(c_all, x), bit)
            hid, seen_hid = up(x)
            grad, seen_grad = back(after(c, seen_grad[1], seen_hid[1]))
            hids.append(hid)
            grads.append(grad)

        hid = jnp.concatenate(hids, steps)
        act = gelu_parts(hid)[0].astype(bf16)
        grad = jnp.concatenate(grads, steps)
        hid, grad = lax.optimization_barrier((hid, grad))
        grad = (grad * gelu_parts(hid)[1]).astype(bf16)

        def gather(v):
            v = gather_chips(v, 1)
            quarter = cut // 2
            firsts, seconds = [], []
            for p in range(2):
                w = gather_chips_last(v[..., p * quarter : (p + 1) * quarter])
                got = swap_core(w)
                firsts.append(jnp.where(core == 0, w, got))
                seconds.append(turn(jnp.where(core == 0, got, w)))
            return lax.optimization_barrier(lax.concatenate(firsts + seconds, steps + 2))

        def gather_chips_last(v):
            return lax.concatenate([v, swap_chip(v, 0)], 0)

        act_all = gather(act)
        grad_all = gather(grad)
        lead = act_all.shape[:-1]

        mixed = jnp.dot(flat(act_all), w_out, preferred_element_type=f32).astype(bf16).reshape(lead + (width,))
        for bit in reversed(range(col_bits)):
            blocks = mixed.shape[steps] // 2
            got = swap_col(lax.slice_in_dim(mixed, blocks, 2 * blocks, axis=steps), bit)
            keep = lax.slice_in_dim(mixed, 0, blocks, axis=steps)
            mixed = (keep.astype(f32) + got.astype(f32)).astype(bf16)
        mixed = flips(mixed, first, 0).reshape(tokens, width)

        grad_w_out = lax.dot_general(
            flat(act_all), flat(c_all), (((0,), (0,)), ((), ())), preferred_element_type=f32
        )
        x_t = lax.optimization_barrier(flat(x_all).T)
        grad_w_in = jnp.dot(x_t, flat(grad_all), preferred_element_type=f32)
        return (mixed, grad_w_in.astype(bf16), grad_w_out.astype(bf16))

    return per_device


def solution(mesh):
    placed = (P("col", "row"), P("row", "col"), P("col", "row"), P("col", "row"))
    return jax.shard_map(
        make(mesh.shape["row"], mesh.shape["col"]),
        mesh=mesh,
        in_specs=placed,
        out_specs=(P("col", "row"), P("row", "col"), P("col", "row")),
        check_vma=False,
    )
```

```python
import jax
import jax.numpy as jnp
from jax import lax
from jax.sharding import PartitionSpec as P

f32 = jnp.float32
bf16 = jnp.bfloat16


def gelu_parts(hidden):
    cdf = 0.5 * (1.0 + jax.scipy.special.erf(hidden * 0.7071067811865476))
    pdf = jnp.exp(-0.5 * hidden * hidden) * 0.3989422804014327
    return (hidden * cdf, cdf + hidden * pdf)


def weight_grad(piece, rows, half, p, into, across):
    quarter = piece.shape[1]
    at = (half * 2 + p) * quarter
    if across:
        out = jnp.dot(rows, piece, preferred_element_type=f32).astype(bf16)
        return lax.dynamic_update_slice(into, out, (0, at))
    out = lax.dot_general(piece, rows, (((0,), (0,)), ((), ())), preferred_element_type=f32).astype(bf16)
    return lax.dynamic_update_slice(into, out, (at, 0))


def down(piece, w_out, half, p, add):
    quarter = piece.shape[1]
    block = lax.dynamic_slice_in_dim(w_out, (half * 2 + p) * quarter, quarter, 0)
    out = jnp.dot(piece, block, preferred_element_type=f32)
    return out if add is None else add + out


def make(n_row, n_col):
    row_bits = n_row.bit_length() - 1
    col_bits = n_col.bit_length() - 1
    first = tuple(range(1, row_bits))
    orders = (first, first[::-1])
    steps = len(first)

    def swap_core(v):
        return lax.ppermute(v, "row", [(i, i ^ 1) for i in range(n_row)])

    def swap_chip(v, step):
        return lax.ppermute(v, "row", [(i, i ^ (1 << orders[i & 1][step])) for i in range(n_row)])

    def swap_col(v, bit):
        return lax.ppermute(v, "col", [(i, i ^ (1 << bit)) for i in range(n_col)])

    def part(v, axis, index):
        return lax.slice_in_dim(v, index, index + 1, axis=axis)

    def flips(v, order, axis):
        me = lax.axis_index("row")
        for k, bit in enumerate(order):
            v = jnp.where((me >> bit) & 1 == 1, jnp.flip(v, axis + k), v)
        return v

    def relative(v):
        v = v.reshape((2,) * steps + (1, v.shape[0] >> steps, v.shape[1]))
        return flips(v, first, 0)

    def turn(v):
        return v.transpose(tuple(range(steps))[::-1] + tuple(range(steps, v.ndim)))

    def after(v, *tokens):
        return lax.optimization_barrier((v,) + tokens)[0]

    def flat(v):
        return v.reshape(-1, v.shape[-1])

    def scatter(parts, *tokens):
        core = lax.axis_index("row") & 1
        second = turn(parts[1])
        got = swap_core(jnp.where(core == 0, second, parts[0]))
        v = jnp.where(core == 0, parts[0], second)
        v = (v.astype(f32) + after(got, *tokens).astype(f32)).astype(bf16)
        seen = [v]
        for k in range(steps):
            got = swap_chip(part(v, k, 1), k)
            seen.append(got)
            v = part(v, k, 0).astype(f32) + got.astype(f32)
            if k + 1 < steps:
                v = v.astype(bf16)
        return v, seen

    def gather_chips(v, stop):
        for k in reversed(range(stop, steps)):
            v = lax.concatenate([v, swap_chip(v, k)], k)
        return v

    def per_device(latents, w_in, w_out, cotangent):
        tokens, width = latents.shape
        cut = w_in.shape[1] // 2
        core = lax.axis_index("row") & 1
        halves = [slice(h * cut, (h + 1) * cut) for h in (0, 1)]
        own_half = core.astype(jnp.int32)
        other_half = 1 - own_half

        def up(x):
            out = [jnp.dot(flat(x), w_in[:, h], preferred_element_type=f32) for h in halves]
            return [v.astype(bf16).reshape(x.shape[:-1] + (cut,)) for v in out]

        def back(c):
            out = [
                lax.dot_general(flat(c), w_out[h], (((1,), (1,)), ((), ())), preferred_element_type=f32)
                for h in halves
            ]
            return [v.astype(bf16).reshape(c.shape[:-1] + (cut,)) for v in out]

        def both(x, c, *tokens):
            n = x.shape[steps]
            v, seen = scatter([lax.concatenate(pair, steps) for pair in zip(up(x), back(c))], *tokens)
            hid = lax.slice_in_dim(v, 0, n, axis=steps)
            grad = lax.slice_in_dim(v, n, 2 * n, axis=steps)
            return hid, grad, seen

        hids, grads = [], []

        def keep(hid, grad):
            hids.append(hid)
            grads.append(grad)

        x_all, c_all = relative(latents), relative(cotangent)
        seen = None
        for bit in reversed(range(col_bits)):
            x, c = swap_col(x_all, bit), swap_col(c_all, bit)
            if seen is None:
                hid, grad, seen = both(x_all, c_all, x)
                keep(hid, grad)
            if bit > 0:
                hid, grad, seen = both(after(x, seen[0]), after(c, seen[0]))
                keep(hid, grad)
            else:
                hid, seen_hid = scatter(up(after(x, seen[0])))
                grad, _ = scatter(back(after(c, seen_hid[0])))
                keep(hid, grad)
            x_all = lax.concatenate([x_all, x], steps)
            c_all = lax.concatenate([c_all, c], steps)

        hid = lax.concatenate(hids, steps)
        act = gelu_parts(hid)[0].astype(bf16)
        grad = lax.concatenate(grads, steps)
        hid, grad = lax.optimization_barrier((hid, grad))
        grad = (grad * gelu_parts(hid)[1]).astype(bf16)

        quarter = cut // 2

        def gather(v):
            v = gather_chips(v, 1)
            out = []
            for p in range(2):
                w = v[..., p * quarter : (p + 1) * quarter]
                w = lax.concatenate([w, swap_chip(w, 0)], 0)
                out.append((own_half, p, flat(w)))
                out.append((other_half, p, flat(swap_core(w))))
            return out

        x_turned, c_turned = turn(x_all), turn(c_all)

        def ordered(plain, turned, half):
            return jnp.where(half == 0, flat(plain), flat(turned))

        x_rows = [lax.optimization_barrier(ordered(x_all, x_turned, h).T) for h in (own_half, other_half)]
        c_rows = [lax.optimization_barrier(ordered(c_all, c_turned, h)) for h in (own_half, other_half)]

        sums = [None, None]
        grad_w_out = jnp.zeros_like(w_out)
        for i, (half, p, piece) in enumerate(gather(act)):
            sums[i & 1] = down(piece, w_out, half, p, sums[i & 1])
            grad_w_out = weight_grad(piece, c_rows[i & 1], half, p, grad_w_out, False)
        grad_w_in = jnp.zeros_like(w_in)
        for i, (half, p, piece) in enumerate(gather(grad)):
            grad_w_in = weight_grad(piece, x_rows[i & 1], half, p, grad_w_in, True)

        sums = [v.reshape(x_all.shape) for v in sums]
        mixed = jnp.where(core == 0, sums[0], sums[1]) + turn(jnp.where(core == 0, sums[1], sums[0]))
        mixed = mixed.astype(bf16)
        for bit in range(col_bits):
            blocks = mixed.shape[steps] // 2
            got = swap_col(lax.slice_in_dim(mixed, blocks, 2 * blocks, axis=steps), bit)
            kept = lax.slice_in_dim(mixed, 0, blocks, axis=steps)
            mixed = (kept.astype(f32) + got.astype(f32)).astype(bf16)
        mixed = flips(mixed, first, 0).reshape(tokens, width)
        return (mixed, grad_w_in, grad_w_out)

    return per_device


def solution(mesh):
    placed = (P("col", "row"), P("row", "col"), P("col", "row"), P("col", "row"))
    return jax.shard_map(
        make(mesh.shape["row"], mesh.shape["col"]),
        mesh=mesh,
        in_specs=placed,
        out_specs=(P("col", "row"), P("row", "col"), P("col", "row")),
        check_vma=False,
    )
```

```python
import jax
import jax.numpy as jnp
from jax import lax
from jax.sharding import PartitionSpec as P

f32 = jnp.float32
bf16 = jnp.bfloat16


def gelu_parts(hidden):
    cdf = 0.5 * (1.0 + jax.scipy.special.erf(hidden * 0.7071067811865476))
    pdf = jnp.exp(-0.5 * hidden * hidden) * 0.3989422804014327
    return (hidden * cdf, cdf + hidden * pdf)


def weight_grad(piece, rows, half, p, into, across):
    quarter = piece.shape[1]
    at = (half * 2 + p) * quarter
    if across:
        out = jnp.dot(rows, piece, preferred_element_type=f32).astype(bf16)
        return lax.dynamic_update_slice(into, out, (0, at))
    out = lax.dot_general(piece, rows, (((0,), (0,)), ((), ())), preferred_element_type=f32).astype(bf16)
    return lax.dynamic_update_slice(into, out, (at, 0))


def down(piece, w_out, half, p, add):
    quarter = piece.shape[1]
    block = lax.dynamic_slice_in_dim(w_out, (half * 2 + p) * quarter, quarter, 0)
    out = jnp.dot(piece, block, preferred_element_type=f32)
    return out if add is None else add + out


def make(n_row, n_col):
    row_bits = n_row.bit_length() - 1
    first = tuple(range(1, row_bits))
    orders = (first, first[::-1])
    steps = len(first)

    def swap_core(v):
        return lax.ppermute(v, "row", [(i, i ^ 1) for i in range(n_row)])

    def swap_chip(v, step):
        return lax.ppermute(v, "row", [(i, i ^ (1 << orders[i & 1][step])) for i in range(n_row)])

    def part(v, axis, index):
        return lax.slice_in_dim(v, index, index + 1, axis=axis)

    def flips(v, order, axis):
        me = lax.axis_index("row")
        for k, bit in enumerate(order):
            v = jnp.where((me >> bit) & 1 == 1, jnp.flip(v, axis + k), v)
        return v

    def relative(v):
        v = v.reshape((2,) * steps + (1, v.shape[0] >> steps, v.shape[1]))
        return flips(v, first, 0)

    def turn(v):
        return v.transpose(tuple(range(steps))[::-1] + tuple(range(steps, v.ndim)))

    def after(v, *tokens):
        return lax.optimization_barrier((v,) + tokens)[0]

    def flat(v):
        return v.reshape(-1, v.shape[-1])

    def scatter(parts, *tokens):
        core = lax.axis_index("row") & 1
        second = turn(parts[1])
        got = swap_core(jnp.where(core == 0, second, parts[0]))
        v = jnp.where(core == 0, parts[0], second)
        v = (v.astype(f32) + after(got, *tokens).astype(f32)).astype(bf16)
        seen = [v]
        for k in range(steps):
            got = swap_chip(part(v, k, 1), k)
            seen.append(got)
            v = part(v, k, 0).astype(f32) + got.astype(f32)
            if k + 1 < steps:
                v = v.astype(bf16)
        return v, seen

    def gather_chips(v, stop):
        for k in reversed(range(stop, steps)):
            v = lax.concatenate([v, swap_chip(v, k)], k)
        return v

    def per_device(latents, w_in, w_out, cotangent):
        tokens, width = latents.shape
        cut = w_in.shape[1] // 2
        core = lax.axis_index("row") & 1
        halves = [slice(h * cut, (h + 1) * cut) for h in (0, 1)]
        own_half = core.astype(jnp.int32)
        other_half = 1 - own_half

        def up(x):
            out = [jnp.dot(flat(x), w_in[:, h], preferred_element_type=f32) for h in halves]
            return [v.astype(bf16).reshape(x.shape[:-1] + (cut,)) for v in out]

        def back(c):
            out = [
                lax.dot_general(flat(c), w_out[h], (((1,), (1,)), ((), ())), preferred_element_type=f32)
                for h in halves
            ]
            return [v.astype(bf16).reshape(c.shape[:-1] + (cut,)) for v in out]

        def both(x, c, *tokens):
            n = x.shape[steps]
            v, seen = scatter([lax.concatenate(pair, steps) for pair in zip(up(x), back(c))], *tokens)
            hid = lax.slice_in_dim(v, 0, n, axis=steps)
            grad = lax.slice_in_dim(v, n, 2 * n, axis=steps)
            return hid, grad, seen

        mine = lax.optimization_barrier(lax.concatenate([relative(latents), relative(cotangent)], steps + 2))
        every = lax.all_gather(mine, "col", axis=steps, tiled=True)

        def rolled(v, by):
            n = v.shape[steps]
            return lax.dynamic_slice_in_dim(lax.concatenate([v, v], steps), by, n, steps)

        here = lax.axis_index("col")
        x_own, c_own = mine[..., :width], mine[..., width:]
        others = lax.slice_in_dim(rolled(every, here), 1, n_col, axis=steps)
        x_others, c_others = others[..., :width], others[..., width:]
        x_all = lax.concatenate([x_own, x_others], steps)
        c_all = lax.concatenate([c_own, c_others], steps)

        hid, grad, seen = both(x_own, c_own)
        hid_others, seen_hid = scatter(up(after(x_others, seen[1])))
        grad_others, seen_grad = scatter(back(after(c_others, seen_hid[0])))
        hids, grads = [hid, hid_others], [grad, grad_others]

        hid = lax.concatenate(hids, steps)
        act = gelu_parts(hid)[0].astype(bf16)
        grad = lax.concatenate(grads, steps)
        hid, grad = lax.optimization_barrier((hid, grad))
        grad = (grad * gelu_parts(hid)[1]).astype(bf16)

        quarter = cut // 2

        def gather(v, p):
            w = v[..., p * quarter : (p + 1) * quarter]
            return lax.concatenate([w, swap_chip(w, 0)], 0)

        x_turned, c_turned = turn(x_all), turn(c_all)

        def ordered(plain, turned, half):
            return jnp.where(half == 0, flat(plain), flat(turned))

        x_rows = [lax.optimization_barrier(ordered(x_all, x_turned, h).T) for h in (own_half, other_half)]
        c_rows = [lax.optimization_barrier(ordered(c_all, c_turned, h)) for h in (own_half, other_half)]

        act = gather_chips(act, 1)
        grad = gather_chips(grad, 1)
        sums = [None, None]
        grad_w_out = jnp.zeros_like(w_out)
        grad_w_in = jnp.zeros_like(w_in)
        acts = [gather(act, p) for p in range(2)]
        grads = [gather(grad, p) for p in range(2)]
        for p in range(2):
            pieces = (acts[p], swap_core(acts[p]))
            for i, half in enumerate((own_half, other_half)):
                sums[i] = down(flat(pieces[i]), w_out, half, p, sums[i])
                grad_w_out = weight_grad(flat(pieces[i]), c_rows[i], half, p, grad_w_out, False)
        grads[1] = after(grads[1], grad_w_out)
        for p in range(2):
            pieces = (grads[p], swap_core(grads[p]))
            for i, half in enumerate((own_half, other_half)):
                grad_w_in = weight_grad(flat(pieces[i]), x_rows[i], half, p, grad_w_in, True)

        sums = [v.reshape(x_all.shape) for v in sums]
        mixed = jnp.where(core == 0, sums[0], sums[1]) + turn(jnp.where(core == 0, sums[1], sums[0]))
        mixed = mixed.astype(bf16)
        mixed = rolled(mixed, (n_col - here) % n_col)
        mixed = lax.psum_scatter(mixed, "col", scatter_dimension=steps, tiled=True)
        mixed = flips(mixed, first, 0).reshape(tokens, width)
        return (mixed, grad_w_in, grad_w_out)

    return per_device


def solution(mesh):
    placed = (P("col", "row"), P("row", "col"), P("col", "row"), P("col", "row"))
    return jax.shard_map(
        make(mesh.shape["row"], mesh.shape["col"]),
        mesh=mesh,
        in_specs=placed,
        out_specs=(P("col", "row"), P("row", "col"), P("col", "row")),
        check_vma=False,
    )
```

```python
import jax
import jax.numpy as jnp
from jax import lax
from jax.sharding import PartitionSpec as P

f32 = jnp.float32
bf16 = jnp.bfloat16


def gelu_parts(hidden):
    cdf = 0.5 * (1.0 + jax.scipy.special.erf(hidden * 0.7071067811865476))
    pdf = jnp.exp(-0.5 * hidden * hidden) * 0.3989422804014327
    return (hidden * cdf, cdf + hidden * pdf)


def terms(plain, turned, w, core, back):
    cut = w.shape[0 if back else 1] // 2
    if back:
        out = [
            lax.dot_general(v, w[h * cut : (h + 1) * cut], (((1,), (1,)), ((), ())), preferred_element_type=f32)
            for h, v in enumerate((plain, turned))
        ]
    else:
        out = [
            jnp.dot(v, w[:, h * cut : (h + 1) * cut], preferred_element_type=f32)
            for h, v in enumerate((plain, turned))
        ]
    out = [v.astype(bf16) for v in out]
    return jnp.where(core == 0, out[0], out[1]), jnp.where(core == 0, out[1], out[0])


def add_and_split(v, got):
    rows = v.shape[0]
    total = (v.astype(f32) + got.astype(f32)).astype(bf16)
    return total[: rows // 2], total[rows // 2 :]


def weight_grad(piece, rows, half, p, into, across):
    quarter = piece.shape[1]
    at = (half * 2 + p) * quarter
    if across:
        out = jnp.dot(rows, piece, preferred_element_type=f32).astype(bf16)
        return lax.dynamic_update_slice(into, out, (0, at))
    out = lax.dot_general(piece, rows, (((0,), (0,)), ((), ())), preferred_element_type=f32).astype(bf16)
    return lax.dynamic_update_slice(into, out, (at, 0))


def down(piece, w_out, half, p, add):
    quarter = piece.shape[1]
    block = lax.dynamic_slice_in_dim(w_out, (half * 2 + p) * quarter, quarter, 0)
    out = jnp.dot(piece, block, preferred_element_type=f32)
    return out if add is None else add + out


def make(n_row, n_col):
    row_bits = n_row.bit_length() - 1
    col_bits = n_col.bit_length() - 1
    first = tuple(range(1, row_bits))
    orders = (first, first[::-1])
    steps = len(first)

    def swap_core(v):
        return lax.ppermute(v, "row", [(i, i ^ 1) for i in range(n_row)])

    def swap_chip(v, step):
        return lax.ppermute(v, "row", [(i, i ^ (1 << orders[i & 1][step])) for i in range(n_row)])

    def swap_col(v, bit):
        return lax.ppermute(v, "col", [(i, i ^ (1 << bit)) for i in range(n_col)])

    def part(v, axis, index):
        return lax.slice_in_dim(v, index, index + 1, axis=axis)

    def flips(v, order, axis):
        me = lax.axis_index("row")
        for k, bit in enumerate(order):
            v = jnp.where((me >> bit) & 1 == 1, jnp.flip(v, axis + k), v)
        return v

    def relative(v):
        v = v.reshape((2,) * steps + (1, v.shape[0] >> steps, v.shape[1]))
        return flips(v, first, 0)

    def turn(v):
        return v.transpose(tuple(range(steps))[::-1] + tuple(range(steps, v.ndim)))

    def after(v, *tokens):
        return lax.optimization_barrier((v,) + tokens)[0]

    def flat(v):
        return v.reshape(-1, v.shape[-1])

    def per_device(latents, w_in, w_out, cotangent):
        tokens, width = latents.shape
        cut = w_in.shape[1] // 2
        core = lax.axis_index("row") & 1
        own_half = core.astype(jnp.int32)
        other_half = 1 - own_half

        taken = []

        def take(got, *also):
            got = after(got, *taken, *also)
            taken[:] = [got]
            return got

        def up(x):
            own, other = terms(flat(x), flat(turn(x)), w_in, own_half, False)
            return own, swap_core(other)

        def back(c):
            own, other = terms(flat(c), flat(turn(c)), w_out, own_half, True)
            return own, swap_core(other)

        def step(keep, got, k):
            keep, send = add_and_split(keep, got)
            return keep, swap_chip(send, k)

        def total(keep, got):
            return (keep.astype(f32) + got.astype(f32)).reshape((1,) * steps + (-1, tokens >> steps, cut))

        def double(v, got):
            return lax.concatenate([v, got], steps)

        def steps_on(flight, begin, end):
            for k in range(begin, end):
                flight = step(flight[0], take(flight[1]), k)
            return flight

        both = lax.concatenate([relative(latents), relative(cotangent)], steps + 2)
        both = double(both, take(swap_col(both, 0)))
        x_all, c_all = both[..., :width], both[..., width:]
        hid = up(x_all)
        grad = back(c_all)
        x_next = swap_col(x_all, 1) if col_bits > 1 else None
        hid = step(hid[0], take(hid[1]), 0)
        grad = step(grad[0], take(grad[1]), 0)
        hids, grads = [], []
        for bit in range(1, col_bits):
            hid = hid[0], take(hid[1])
            x = take(x_next)
            grad = grad[0], take(grad[1])
            hid = step(*hid, 1) if steps > 1 else hid
            hid_new = up(after(x, grad[1]))
            grad = step(*grad, 1) if steps > 1 else grad
            c_next = swap_col(after(c_all, x), bit)
            x_all = double(x_all, x)
            x_next = swap_col(x_all, bit + 1) if bit + 1 < col_bits else None
            hid_new = step(hid_new[0], take(hid_new[1]), 0)
            hid = steps_on(hid, 2, steps)
            hids.append(total(hid[0], take(hid[1])))
            grad = steps_on(grad, 2, steps)
            grads.append(total(grad[0], take(grad[1])))
            c = take(c_next)
            c_all = double(c_all, c)
            hid = hid_new[0], take(hid_new[1])
            grad = back(after(c, hid[1]))
            if bit + 1 < col_bits:
                grad = step(grad[0], take(grad[1]), 0)
        if col_bits > 1:
            hid = step(*hid, 1)
            grad = step(grad[0], take(grad[1]), 0)
        hid = steps_on(hid, 2, steps)

        hids.append(total(hid[0], take(hid[1])))
        hid = lax.concatenate(hids, steps)
        act = gelu_parts(hid)[0].astype(bf16)

        def doubled(flight, k):
            return lax.concatenate([flight[0], take(flight[1])], k)

        def chips(v, begin, end):
            flight = v, swap_chip(v, end - 1)
            for k in reversed(range(begin, end - 1)):
                v = doubled(flight, k + 1)
                flight = v, swap_chip(v, k)
            return flight

        quarter = cut // 2

        def quarters(v):
            return [v[..., p * quarter : (p + 1) * quarter] for p in range(2)]

        act = chips(act, 1, steps)
        grad = steps_on(grad, 1, steps)
        act = quarters(doubled(act, 1))
        acts = [(v, swap_chip(v, 0)) for v in act]
        grads.append(total(grad[0], take(grad[1])))
        grad = lax.concatenate(grads, steps)
        hid, grad = lax.optimization_barrier((hid, grad))
        grad = chips((grad * gelu_parts(hid)[1]).astype(bf16), 1, steps)

        x_turned, c_turned = turn(x_all), turn(c_all)

        def ordered(plain, turned, half):
            return jnp.where(half == 0, flat(plain), flat(turned))

        x_rows = [lax.optimization_barrier(ordered(x_all, x_turned, h).T) for h in (own_half, other_half)]
        c_rows = [lax.optimization_barrier(ordered(c_all, c_turned, h)) for h in (own_half, other_half)]

        acts[0] = doubled(acts[0], 0)
        acts[0] = acts[0], swap_core(acts[0])
        acts[1] = doubled(acts[1], 0)
        acts[1] = acts[1], swap_core(acts[1])
        acts[0] = acts[0][0], take(acts[0][1])
        grad = quarters(doubled(grad, 1))
        grads = [(v, swap_chip(v, 0)) for v in grad]
        acts[1] = acts[1][0], take(acts[1][1])

        sums = [None, None]
        for p in range(2):
            for i, half in enumerate((own_half, other_half)):
                sums[i] = down(flat(acts[p][i]), w_out, half, p, sums[i])
        sums = [v.reshape(x_all.shape) for v in sums]
        mixed = jnp.where(core == 0, sums[0], sums[1]) + turn(jnp.where(core == 0, sums[1], sums[0]))
        mixed = mixed.astype(bf16)

        def halve(mixed, bit):
            blocks = mixed.shape[steps]
            mixed = mixed.reshape(mixed.shape[:steps] + (blocks // 2, 2) + mixed.shape[steps + 1 :])
            return (
                lax.index_in_dim(mixed, 0, steps + 1, False),
                swap_col(lax.index_in_dim(mixed, 1, steps + 1, False), bit),
            )

        def merged(flight):
            return (flight[0].astype(f32) + take(flight[1]).astype(f32)).astype(bf16)

        mixed = halve(mixed, 0)
        grad_w_out = jnp.zeros_like(w_out)
        for i, half in enumerate((own_half, other_half)):
            grad_w_out = weight_grad(flat(acts[0][i]), c_rows[i], half, 0, grad_w_out, False)
        grads[0] = lax.concatenate([grads[0][0], take(grads[0][1], grad_w_out)], 0)
        grads[0] = grads[0], swap_core(grads[0])
        for bit in range(1, col_bits):
            mixed = halve(merged(mixed), bit)
        for i, half in enumerate((own_half, other_half)):
            grad_w_out = weight_grad(flat(acts[1][i]), c_rows[i], half, 1, grad_w_out, False)
        grads[1] = lax.concatenate([grads[1][0], take(grads[1][1], grad_w_out)], 0)
        grads[1] = grads[1], swap_core(grads[1])
        grads[0] = grads[0][0], take(grads[0][1])
        grad_w_in = jnp.zeros_like(w_in)
        for p, i in ((0, 0), (0, 1), (1, 0)):
            grad_w_in = weight_grad(flat(grads[p][i]), x_rows[i], (own_half, other_half)[i], p, grad_w_in, True)
        mixed = flips(merged(mixed), first, 0).reshape(tokens, width)
        grad_w_in = weight_grad(flat(take(grads[1][1])), x_rows[1], other_half, 1, grad_w_in, True)
        return (mixed, grad_w_in, grad_w_out)

    return per_device


def solution(mesh):
    placed = (P("col", "row"), P("row", "col"), P("col", "row"), P("col", "row"))
    return jax.shard_map(
        make(mesh.shape["row"], mesh.shape["col"]),
        mesh=mesh,
        in_specs=placed,
        out_specs=(P("col", "row"), P("row", "col"), P("col", "row")),
        check_vma=False,
    )
```

```python
import jax
import jax.numpy as jnp
from jax import lax
from jax.sharding import PartitionSpec as P

f32 = jnp.float32
bf16 = jnp.bfloat16


def gelu_parts(hidden):
    cdf = 0.5 * (1.0 + jax.scipy.special.erf(hidden * 0.7071067811865476))
    pdf = jnp.exp(-0.5 * hidden * hidden) * 0.3989422804014327
    return (hidden * cdf, cdf + hidden * pdf)


def add_and_split(v, got):
    rows = v.shape[0]
    total = (v.astype(f32) + got.astype(f32)).astype(bf16)
    return total[: rows // 2], total[rows // 2 :]


def weight_grad(piece, rows, half, p, into, across):
    quarter = piece.shape[1]
    at = (half * 2 + p) * quarter
    if across:
        out = jnp.dot(rows, piece, preferred_element_type=f32).astype(bf16)
        return lax.dynamic_update_slice(into, out, (0, at))
    out = lax.dot_general(piece, rows, (((0,), (0,)), ((), ())), preferred_element_type=f32).astype(bf16)
    return lax.dynamic_update_slice(into, out, (at, 0))


def make(n_row, n_col):
    row_bits = n_row.bit_length() - 1
    col_bits = n_col.bit_length() - 1
    first = tuple(range(1, row_bits))
    orders = (first, first[::-1])
    steps = len(first)

    def swap_core(v):
        return lax.ppermute(v, "row", [(i, i ^ 1) for i in range(n_row)])

    def swap_chip(v, step):
        return lax.ppermute(v, "row", [(i, i ^ (1 << orders[i & 1][step])) for i in range(n_row)])

    def part(v, axis, index):
        return lax.slice_in_dim(v, index, index + 1, axis=axis)

    def flips(v, order, axis):
        me = lax.axis_index("row")
        for k, bit in enumerate(order):
            v = jnp.where((me >> bit) & 1 == 1, jnp.flip(v, axis + k), v)
        return v

    def relative(v):
        v = v.reshape((2,) * steps + (1, v.shape[0] >> steps, v.shape[1]))
        return flips(v, first, 0)

    def turn(v):
        return v.transpose(tuple(range(steps))[::-1] + tuple(range(steps, v.ndim)))

    def after(v, *tokens):
        return lax.optimization_barrier((v,) + tokens)[0]

    def flat(v):
        return v.reshape(-1, v.shape[-1])

    def per_device(latents, w_in, w_out, cotangent):
        tokens, width = latents.shape
        cut = w_in.shape[1] // 2
        core = lax.axis_index("row") & 1
        own_half = core.astype(jnp.int32)
        other_half = 1 - own_half

        taken = []

        def take(got, *also):
            got = after(got, *taken, *also)
            taken[:] = [got]
            return got

        def halves(w, axis):
            return lax.optimization_barrier(
                tuple(lax.dynamic_slice_in_dim(w, h * cut, cut, axis) for h in (own_half, other_half))
            )

        def ordered(v):
            plain, turned = flat(v), flat(turn(v))
            return jnp.where(core == 0, plain, turned), jnp.where(core == 0, turned, plain)

        w_in_own, w_in_other = halves(w_in, 1)
        w_out_own, w_out_other = halves(w_out, 0)

        def up(x):
            own, other = ordered(x)
            got = swap_core(jnp.dot(other, w_in_other, preferred_element_type=f32).astype(bf16))
            return jnp.dot(own, w_in_own, preferred_element_type=f32).astype(bf16), got

        def back(c):
            own, other = ordered(c)
            dims = (((1,), (1,)), ((), ()))
            got = swap_core(lax.dot_general(other, w_out_other, dims, preferred_element_type=f32).astype(bf16))
            return lax.dot_general(own, w_out_own, dims, preferred_element_type=f32).astype(bf16), got

        def step(keep, got, k):
            keep, send = add_and_split(keep, got)
            return keep, swap_chip(send, k)

        def total(keep, got):
            return (keep.astype(f32) + got.astype(f32)).reshape((1,) * steps + (-1, tokens >> steps, cut))

        def steps_on(flight, begin, end):
            for k in range(begin, end):
                flight = step(flight[0], take(flight[1]), k)
            return flight

        def reach(v, distance):
            return lax.ppermute(v, "col", [(i, i ^ distance) for i in range(n_col)])

        x_own, c_own = relative(latents), relative(cotangent)
        near = reach(lax.concatenate([x_own, c_own], steps + 2), 1)
        x_far = [reach(x_own, d) for d in range(2, n_col)]
        x_far, near = lax.optimization_barrier((x_far, near))
        x_near = lax.concatenate([x_own, near[..., :width]], steps)
        c_near = lax.concatenate([c_own, near[..., width:]], steps)
        x_far = lax.concatenate(x_far, steps)
        x_all = lax.concatenate([x_near, x_far], steps)
        hid_near, hid_far, grad_near = up(x_near), up(x_far), back(c_near)
        x_rows = [lax.optimization_barrier(v.T) for v in ordered(x_all)]

        hid_near = step(hid_near[0], take(hid_near[1]), 0)
        hid_far = step(hid_far[0], take(hid_far[1]), 0)
        grad_near = grad_near[0], take(grad_near[1])
        c_far = [reach(after(c_own, x_far), d) for d in range(2, n_col)]
        hid_near = step(hid_near[0], take(hid_near[1], *x_rows), 1)
        grad_near = step(*grad_near, 0)
        hid_far = step(hid_far[0], take(hid_far[1]), 1)
        hid_near = steps_on(hid_near, 2, steps)
        hids = [total(hid_near[0], take(hid_near[1]))]
        c_far = lax.concatenate([take(v) for v in c_far], steps)
        grad_far = back(c_far)
        c_all = lax.concatenate([c_near, c_far], steps)
        c_rows = [lax.optimization_barrier(v) for v in ordered(c_all)]
        grad_near = step(grad_near[0], take(grad_near[1]), 1)
        hid_far = steps_on(hid_far, 2, steps)
        hids.append(total(hid_far[0], take(hid_far[1])))
        hid = lax.concatenate(hids, steps)
        act = gelu_parts(hid)[0].astype(bf16)

        def doubled(flight, k):
            return lax.concatenate([flight[0], take(flight[1])], k)

        def chips(v, begin, end):
            flight = v, swap_chip(v, end - 1)
            for k in reversed(range(begin, end - 1)):
                v = doubled(flight, k + 1)
                flight = v, swap_chip(v, k)
            return flight

        quarter = cut // 2

        def quarters(v):
            return [v[..., p * quarter : (p + 1) * quarter] for p in range(2)]

        act = chips(act, 1, steps)
        grad_far = step(grad_far[0], take(grad_far[1]), 0)
        grad_near = steps_on(grad_near, 2, steps)
        grads = [total(grad_near[0], take(grad_near[1], *c_rows))]
        act = quarters(doubled(act, 1))
        acts = [(v, swap_chip(v, 0)) for v in act]
        grad_far = step(grad_far[0], take(grad_far[1]), 1)
        acts[0] = doubled(acts[0], 0)
        acts[0] = acts[0], swap_core(acts[0])
        grad_far = steps_on(grad_far, 2, steps)
        grads.append(total(grad_far[0], take(grad_far[1])))
        grad = lax.concatenate(grads, steps)
        hid, grad = lax.optimization_barrier((hid, grad))
        grad = chips((grad * gelu_parts(hid)[1]).astype(bf16), 1, steps)
        acts[1] = doubled(acts[1], 0)
        acts[1] = acts[1], swap_core(acts[1])
        acts[0] = acts[0][0], take(acts[0][1])
        acts[1] = acts[1][0], take(acts[1][1])

        sums = []
        for i, w in enumerate((w_out_own, w_out_other)):
            parts = [
                jnp.dot(flat(acts[p][i]), w[p * quarter : (p + 1) * quarter], preferred_element_type=f32)
                for p in range(2)
            ]
            sums.append((parts[0] + parts[1]).reshape(x_all.shape))
        mixed = jnp.where(core == 0, sums[0], sums[1]) + turn(jnp.where(core == 0, sums[1], sums[0]))
        mixed = mixed.astype(bf16)

        def halve(mixed, bit):
            blocks = mixed.shape[steps]
            mixed = mixed.reshape(mixed.shape[:steps] + (blocks // 2, 2) + mixed.shape[steps + 1 :])
            return (
                lax.index_in_dim(mixed, 0, steps + 1, False),
                reach(lax.index_in_dim(mixed, 1, steps + 1, False), 1 << bit),
            )

        def merged(flight):
            return (flight[0].astype(f32) + take(flight[1]).astype(f32)).astype(bf16)

        mixed = halve(mixed, 0)
        grad = quarters(doubled(grad, 1))
        grads = [(v, swap_chip(v, 0)) for v in grad]
        grad_w_out = jnp.zeros_like(w_out)
        for i, half in enumerate((own_half, other_half)):
            grad_w_out = weight_grad(flat(acts[0][i]), c_rows[i], half, 0, grad_w_out, False)
        grads[0] = lax.concatenate([grads[0][0], take(grads[0][1], grad_w_out)], 0)
        grads[0] = grads[0], swap_core(grads[0])
        for bit in range(1, col_bits):
            mixed = halve(merged(mixed), bit)
        for i, half in enumerate((own_half, other_half)):
            grad_w_out = weight_grad(flat(acts[1][i]), c_rows[i], half, 1, grad_w_out, False)
        grads[1] = lax.concatenate([grads[1][0], take(grads[1][1], grad_w_out)], 0)
        grads[1] = grads[1], swap_core(grads[1])
        grads[0] = grads[0][0], take(grads[0][1])
        grad_w_in = jnp.zeros_like(w_in)
        for p, i in ((0, 0), (0, 1), (1, 0)):
            grad_w_in = weight_grad(flat(grads[p][i]), x_rows[i], (own_half, other_half)[i], p, grad_w_in, True)
        mixed = flips(merged(mixed), first, 0).reshape(tokens, width)
        grad_w_in = weight_grad(flat(take(grads[1][1])), x_rows[1], other_half, 1, grad_w_in, True)
        return (mixed, grad_w_in, grad_w_out)

    return per_device


def solution(mesh):
    placed = (P("col", "row"), P("row", "col"), P("col", "row"), P("col", "row"))
    return jax.shard_map(
        make(mesh.shape["row"], mesh.shape["col"]),
        mesh=mesh,
        in_specs=placed,
        out_specs=(P("col", "row"), P("row", "col"), P("col", "row")),
        check_vma=False,
    )
```

```python
import jax
import jax.numpy as jnp
from jax import lax
from jax.sharding import PartitionSpec as P

f32 = jnp.float32
bf16 = jnp.bfloat16


def gelu_parts(hidden):
    cdf = 0.5 * (1.0 + jax.scipy.special.erf(hidden * 0.7071067811865476))
    pdf = jnp.exp(-0.5 * hidden * hidden) * 0.3989422804014327
    return (hidden * cdf, cdf + hidden * pdf)


def add_and_split(v, got):
    rows = v.shape[0]
    total = (v.astype(f32) + got.astype(f32)).astype(bf16)
    return total[: rows // 2], total[rows // 2 :]


def weight_grad(piece, rows, half, p, into, across):
    quarter = piece.shape[1]
    at = (half * 2 + p) * quarter
    if across:
        out = jnp.dot(rows, piece, preferred_element_type=f32).astype(bf16)
        return lax.dynamic_update_slice(into, out, (0, at))
    out = lax.dot_general(piece, rows, (((0,), (0,)), ((), ())), preferred_element_type=f32).astype(bf16)
    return lax.dynamic_update_slice(into, out, (at, 0))


def make(n_row, n_col):
    row_bits = n_row.bit_length() - 1
    col_bits = n_col.bit_length() - 1
    first = tuple(range(1, row_bits))
    orders = (first, first[::-1])
    steps = len(first)

    def swap_core(v):
        return lax.ppermute(v, "row", [(i, i ^ 1) for i in range(n_row)])

    def swap_chip(v, step):
        return lax.ppermute(v, "row", [(i, i ^ (1 << orders[i & 1][step])) for i in range(n_row)])

    def part(v, axis, index):
        return lax.slice_in_dim(v, index, index + 1, axis=axis)

    def flips(v, order, axis):
        me = lax.axis_index("row")
        for k, bit in enumerate(order):
            v = jnp.where((me >> bit) & 1 == 1, jnp.flip(v, axis + k), v)
        return v

    def relative(v):
        v = v.reshape((2,) * steps + (1, v.shape[0] >> steps, v.shape[1]))
        return flips(v, first, 0)

    def turn(v):
        return v.transpose(tuple(range(steps))[::-1] + tuple(range(steps, v.ndim)))

    def after(v, *tokens):
        return lax.optimization_barrier((v,) + tokens)[0]

    def flat(v):
        return v.reshape(-1, v.shape[-1])

    def per_device(latents, w_in, w_out, cotangent):
        tokens, width = latents.shape
        cut = w_in.shape[1] // 2
        core = lax.axis_index("row") & 1
        own_half = core.astype(jnp.int32)
        other_half = 1 - own_half

        taken = []

        def take(got, *also):
            got = after(got, *taken, *also)
            taken[:] = [got]
            return got

        def ordered(v):
            plain, turned = flat(v), flat(turn(v))
            return jnp.where(core == 0, plain, turned), jnp.where(core == 0, turned, plain)

        def by_core(parts):
            own = jnp.where(core == 0, parts[0], parts[1])
            return own, swap_core(jnp.where(core == 0, parts[1], parts[0]))

        def up_parts(x):
            return [
                jnp.dot(v, w_in[:, h * cut : (h + 1) * cut], preferred_element_type=f32).astype(bf16)
                for h, v in enumerate((flat(x), flat(turn(x))))
            ]

        def up(x):
            return by_core(up_parts(x))

        def back(c):
            dims = (((1,), (1,)), ((), ()))
            return by_core(
                [
                    lax.dot_general(v, w_out[h * cut : (h + 1) * cut], dims, preferred_element_type=f32).astype(bf16)
                    for h, v in enumerate((flat(c), flat(turn(c))))
                ]
            )

        def step(keep, got, k):
            keep, send = add_and_split(keep, got)
            return keep, swap_chip(send, k)

        def total(keep, got):
            return (keep.astype(f32) + got.astype(f32)).reshape((1,) * steps + (-1, tokens >> steps, cut))

        def steps_on(flight, begin, end):
            for k in range(begin, end):
                flight = step(flight[0], take(flight[1]), k)
            return flight

        def reach(v, distance):
            return lax.ppermute(v, "col", [(i, i ^ distance) for i in range(n_col)])

        x_own, c_own = relative(latents), relative(cotangent)
        near = take(reach(lax.concatenate([x_own, c_own], steps + 2), 1))
        x_near = lax.concatenate([x_own, near[..., :width]], steps)
        c_near = lax.concatenate([c_own, near[..., width:]], steps)
        hid_near, grad_near = up(x_near), back(c_near)
        hid_near = step(hid_near[0], take(hid_near[1]), 0)
        grad_near = step(grad_near[0], take(grad_near[1]), 0)
        hid_near = hid_near[0], take(hid_near[1])
        x_far = lax.concatenate([take(reach(x_own, d)) for d in range(2, n_col)], steps)
        grad_near = grad_near[0], take(grad_near[1])
        hid_near = step(*hid_near, 1)
        grad_near = step(*grad_near, 1)
        hid_far = up(after(x_far, grad_near[0]))
        c_far = [reach(after(c_own, x_far), d) for d in range(2, n_col)]
        hid_far = step(hid_far[0], take(hid_far[1]), 0)
        hid_near = steps_on(hid_near, 2, steps)
        hids = [total(hid_near[0], take(hid_near[1]))]
        x_all = lax.concatenate([x_near, x_far], steps)
        x_rows = [lax.optimization_barrier(v.T) for v in ordered(x_all)]
        grad_near = steps_on(grad_near, 2, steps)
        grads = [total(grad_near[0], take(grad_near[1], *x_rows))]
        c_far = lax.concatenate([take(v) for v in c_far], steps)
        c_all = lax.concatenate([c_near, c_far], steps)
        c_rows = [lax.optimization_barrier(v) for v in ordered(c_all)]
        hid_far = step(hid_far[0], take(hid_far[1]), 1)
        grad_far = back(after(c_far, hid_far[0]))
        hid_far = steps_on(hid_far, 2, steps)
        hids.append(total(hid_far[0], take(hid_far[1])))
        hid = lax.concatenate(hids, steps)
        act = gelu_parts(hid)[0].astype(bf16)

        def doubled(flight, k):
            return lax.concatenate([flight[0], take(flight[1])], k)

        def chips(v, begin, end):
            flight = v, swap_chip(v, end - 1)
            for k in reversed(range(begin, end - 1)):
                v = doubled(flight, k + 1)
                flight = v, swap_chip(v, k)
            return flight

        quarter = cut // 2

        def quarters(v):
            return [v[..., p * quarter : (p + 1) * quarter] for p in range(2)]

        act = chips(act, 1, steps)
        grad_far = step(grad_far[0], take(grad_far[1]), 0)
        grad_far = grad_far[0], take(grad_far[1], *c_rows)
        act = quarters(doubled(act, 1))
        grad_far = step(*grad_far, 1)
        acts = [(v, swap_chip(v, 0)) for v in act]
        grad_far = steps_on(grad_far, 2, steps)
        grads.append(total(grad_far[0], take(grad_far[1])))
        grad = lax.concatenate(grads, steps)
        hid, grad = lax.optimization_barrier((hid, grad))
        grad = chips((grad * gelu_parts(hid)[1]).astype(bf16), 1, steps)
        acts = [doubled(v, 0) for v in acts]
        acts = [(v, swap_core(v)) for v in acts]
        grad = quarters(doubled(grad, 1))
        grads = [(v, swap_chip(v, 0)) for v in grad]
        acts = [(v, take(got)) for v, got in acts]

        sums = []
        for i, half in enumerate((own_half, other_half)):
            parts = []
            for p in range(2):
                w = lax.dynamic_slice_in_dim(w_out, (half * 2 + p) * quarter, quarter, 0)
                parts.append(jnp.dot(flat(acts[p][i]), w, preferred_element_type=f32))
            sums.append((parts[0] + parts[1]).reshape(x_all.shape))
        mixed = jnp.where(core == 0, sums[0], sums[1]) + turn(jnp.where(core == 0, sums[1], sums[0]))
        mixed = mixed.astype(bf16)

        def halve(mixed, bit):
            blocks = mixed.shape[steps]
            mixed = mixed.reshape(mixed.shape[:steps] + (blocks // 2, 2) + mixed.shape[steps + 1 :])
            return (
                lax.index_in_dim(mixed, 0, steps + 1, False),
                reach(lax.index_in_dim(mixed, 1, steps + 1, False), 1 << bit),
            )

        def merged(flight, *also):
            return (flight[0].astype(f32) + take(flight[1], *also).astype(f32)).astype(bf16)

        mixed = halve(mixed, 0)
        grad_w_in = lax.optimization_barrier(jnp.zeros_like(w_in))
        grad_w_out = jnp.zeros_like(w_out)
        for i, half in enumerate((own_half, other_half)):
            grad_w_out = weight_grad(flat(acts[0][i]), c_rows[i], half, 0, grad_w_out, False)
        grads[0] = lax.concatenate([grads[0][0], take(grads[0][1], mixed[0], grad_w_in, grad_w_out)], 0)
        grads[0] = grads[0], swap_core(grads[0])
        for bit in range(1, col_bits):
            mixed = halve(merged(mixed), bit)
        for i, half in enumerate((own_half, other_half)):
            grad_w_out = weight_grad(flat(acts[1][i]), c_rows[i], half, 1, grad_w_out, False)
        grads[1] = lax.concatenate([grads[1][0], take(grads[1][1])], 0)
        grads[1] = grads[1], swap_core(grads[1])
        grads[0] = grads[0][0], take(grads[0][1], grad_w_out)
        for p, i in ((0, 0), (0, 1), (1, 0)):
            grad_w_in = weight_grad(flat(grads[p][i]), x_rows[i], (own_half, other_half)[i], p, grad_w_in, True)
        mixed = flips(merged(mixed, grad_w_in), first, 0).reshape(tokens, width)
        grad_w_in = weight_grad(flat(take(grads[1][1])), x_rows[1], other_half, 1, grad_w_in, True)
        return (mixed, grad_w_in, grad_w_out)

    return per_device


def solution(mesh):
    placed = (P("col", "row"), P("row", "col"), P("col", "row"), P("col", "row"))
    return jax.shard_map(
        make(mesh.shape["row"], mesh.shape["col"]),
        mesh=mesh,
        in_specs=placed,
        out_specs=(P("col", "row"), P("row", "col"), P("col", "row")),
        check_vma=False,
    )
```

```python
import jax
import jax.numpy as jnp
from jax import lax
from jax.sharding import PartitionSpec as P

f32 = jnp.float32
bf16 = jnp.bfloat16


def gelu_parts(hidden):
    cdf = 0.5 * (1.0 + jax.scipy.special.erf(hidden * 0.7071067811865476))
    pdf = jnp.exp(-0.5 * hidden * hidden) * 0.3989422804014327
    return (hidden * cdf, cdf + hidden * pdf)


def add_and_split(v, got):
    rows = v.shape[0]
    total = (v.astype(f32) + got.astype(f32)).astype(bf16)
    return total[: rows // 2], total[rows // 2 :]


def weight_grad(piece, rows, half, p, into, across):
    quarter = piece.shape[1]
    at = (half * 2 + p) * quarter
    if across:
        out = jnp.dot(rows, piece, preferred_element_type=f32).astype(bf16)
        return lax.dynamic_update_slice(into, out, (0, at))
    out = lax.dot_general(piece, rows, (((0,), (0,)), ((), ())), preferred_element_type=f32).astype(bf16)
    return lax.dynamic_update_slice(into, out, (at, 0))


def make(n_row, n_col):
    row_bits = n_row.bit_length() - 1
    col_bits = n_col.bit_length() - 1
    first = tuple(range(1, row_bits))
    orders = (first, first[::-1])
    steps = len(first)

    def swap_core(v):
        return lax.ppermute(v, "row", [(i, i ^ 1) for i in range(n_row)])

    def swap_chip(v, step):
        return lax.ppermute(v, "row", [(i, i ^ (1 << orders[i & 1][step])) for i in range(n_row)])

    def part(v, axis, index):
        return lax.slice_in_dim(v, index, index + 1, axis=axis)

    def flips(v, order, axis):
        me = lax.axis_index("row")
        for k, bit in enumerate(order):
            v = jnp.where((me >> bit) & 1 == 1, jnp.flip(v, axis + k), v)
        return v

    def relative(v):
        v = v.reshape((2,) * steps + (1, v.shape[0] >> steps, v.shape[1]))
        return flips(v, first, 0)

    def turn(v):
        return v.transpose(tuple(range(steps))[::-1] + tuple(range(steps, v.ndim)))

    def after(v, *tokens):
        return lax.optimization_barrier((v,) + tokens)[0]

    def flat(v):
        return v.reshape(-1, v.shape[-1])

    def per_device(latents, w_in, w_out, cotangent):
        tokens, width = latents.shape
        cut = w_in.shape[1] // 2
        core = lax.axis_index("row") & 1
        own_half = core.astype(jnp.int32)
        other_half = 1 - own_half

        taken = []

        def take(got, *also):
            got = after(got, *taken, *also)
            taken[:] = [got]
            return got

        def ordered(v):
            plain, turned = flat(v), flat(turn(v))
            return jnp.where(core == 0, plain, turned), jnp.where(core == 0, turned, plain)

        def by_core(parts):
            own = jnp.where(core == 0, parts[0], parts[1])
            return own, swap_core(jnp.where(core == 0, parts[1], parts[0]))

        def up_parts(x):
            return [
                jnp.dot(v, w_in[:, h * cut : (h + 1) * cut], preferred_element_type=f32).astype(bf16)
                for h, v in enumerate((flat(x), flat(turn(x))))
            ]

        def up(x):
            return by_core(up_parts(x))

        def back(c):
            dims = (((1,), (1,)), ((), ()))
            return by_core(
                [
                    lax.dot_general(v, w_out[h * cut : (h + 1) * cut], dims, preferred_element_type=f32).astype(bf16)
                    for h, v in enumerate((flat(c), flat(turn(c))))
                ]
            )

        def step(keep, got, k):
            keep, send = add_and_split(keep, got)
            return keep, swap_chip(send, k)

        def total(keep, got):
            return (keep.astype(f32) + got.astype(f32)).reshape((1,) * steps + (-1, tokens >> steps, cut))

        def steps_on(flight, begin, end):
            for k in range(begin, end):
                flight = step(flight[0], take(flight[1]), k)
            return flight

        def reach(v, distance):
            return lax.ppermute(v, "col", [(i, i ^ distance) for i in range(n_col)])

        x_own, c_own = relative(latents), relative(cotangent)
        blank = lax.slice(flat(x_own), (0, 0), (1, 1)) * 0
        grad_w_in, grad_w_out = lax.optimization_barrier(
            (jnp.broadcast_to(blank, w_in.shape), jnp.broadcast_to(blank, w_out.shape))
        )
        near = take(reach(lax.concatenate([x_own, c_own], steps + 2), 1), grad_w_in, grad_w_out)
        x_near = lax.concatenate([x_own, near[..., :width]], steps)
        c_near = lax.concatenate([c_own, near[..., width:]], steps)
        hid_near, grad_near = up(x_near), back(c_near)
        hid_near = step(hid_near[0], take(hid_near[1]), 0)
        grad_near = step(grad_near[0], take(grad_near[1]), 0)
        hid_near = hid_near[0], take(hid_near[1])
        x_far = lax.concatenate([take(reach(x_own, d)) for d in range(2, n_col)], steps)
        grad_near = grad_near[0], take(grad_near[1])
        x_far = after(x_far, grad_near[1])
        hid_near = step(*hid_near, 1)
        grad_near = step(*grad_near, 1)
        hid_far = up(x_far)
        c_far = [reach(after(c_own, x_far), d) for d in range(2, n_col)]
        hid_far = step(hid_far[0], take(hid_far[1]), 0)
        hid_near = steps_on(hid_near, 2, steps)
        hids = [total(hid_near[0], take(hid_near[1]))]
        x_all = lax.concatenate([x_near, x_far], steps)
        x_rows = [lax.optimization_barrier(v.T) for v in ordered(x_all)]
        grad_near = steps_on(grad_near, 2, steps)
        grads = [total(grad_near[0], take(grad_near[1], *x_rows))]
        hid_far = step(hid_far[0], take(hid_far[1]), 1)
        c_far = lax.concatenate([take(v) for v in c_far], steps)
        c_all = lax.concatenate([c_near, c_far], steps)
        c_rows = [lax.optimization_barrier(v) for v in ordered(c_all)]
        grad_far = back(c_far)
        hid_far = steps_on(hid_far, 2, steps)
        hids.append(total(hid_far[0], take(hid_far[1])))
        hid = lax.concatenate(hids, steps)
        act = gelu_parts(hid)[0].astype(bf16)

        def doubled(flight, k):
            return lax.concatenate([flight[0], take(flight[1])], k)

        def chips(v, begin, end):
            flight = v, swap_chip(v, end - 1)
            for k in reversed(range(begin, end - 1)):
                v = doubled(flight, k + 1)
                flight = v, swap_chip(v, k)
            return flight

        quarter = cut // 2

        def quarters(v):
            return [v[..., p * quarter : (p + 1) * quarter] for p in range(2)]

        act = chips(act, 1, steps)
        grad_far = step(grad_far[0], take(grad_far[1]), 0)
        grad_far = grad_far[0], take(grad_far[1], *c_rows)
        act = quarters(doubled(act, 1))
        grad_far = step(*grad_far, 1)
        acts = [(v, swap_chip(v, 0)) for v in act]
        grad_far = steps_on(grad_far, 2, steps)
        grads.append(total(grad_far[0], take(grad_far[1])))
        grad = lax.concatenate(grads, steps)
        hid, grad = lax.optimization_barrier((hid, grad))
        grad = chips((grad * gelu_parts(hid)[1]).astype(bf16), 1, steps)
        def down(v, half, p):
            w = lax.dynamic_slice_in_dim(w_out, (half * 2 + p) * quarter, quarter, 0)
            return jnp.dot(flat(v), w, preferred_element_type=f32)

        own = doubled(acts[0], 0)
        got = [swap_core(own)]
        sums = [down(own, own_half, 0)]
        grad_w_out = weight_grad(flat(own), c_rows[0], own_half, 0, grad_w_out, False)
        own = lax.concatenate([acts[1][0], take(acts[1][1], sums[0], grad_w_out)], 0)
        got.append(swap_core(own))
        grad = quarters(doubled(grad, 1))
        grads = [(v, swap_chip(v, 0)) for v in grad]
        got[0] = take(got[0])
        sums.append(down(got[0], other_half, 0))
        grad_w_out = weight_grad(flat(got[0]), c_rows[1], other_half, 0, grad_w_out, False)
        got[1] = take(got[1])
        sums[0] = (sums[0] + down(own, own_half, 1)).reshape(x_all.shape)
        sums[1] = (sums[1] + down(got[1], other_half, 1)).reshape(x_all.shape)
        mixed = jnp.where(core == 0, sums[0], sums[1]) + turn(jnp.where(core == 0, sums[1], sums[0]))
        mixed = mixed.astype(bf16)

        def halve(mixed, bit):
            blocks = mixed.shape[steps]
            mixed = mixed.reshape(mixed.shape[:steps] + (blocks // 2, 2) + mixed.shape[steps + 1 :])
            return (
                lax.index_in_dim(mixed, 0, steps + 1, False),
                reach(lax.index_in_dim(mixed, 1, steps + 1, False), 1 << bit),
            )

        def merged(flight, *also):
            return (flight[0].astype(f32) + take(flight[1], *also).astype(f32)).astype(bf16)

        grads[0] = lax.concatenate([grads[0][0], take(grads[0][1], mixed)], 0)
        mixed = halve(mixed, 0)
        grads[0] = grads[0], swap_core(grads[0])
        grad_w_out = weight_grad(flat(own), c_rows[0], own_half, 1, grad_w_out, False)
        grad_w_out = weight_grad(flat(got[1]), c_rows[1], other_half, 1, grad_w_out, False)
        for bit in range(1, col_bits):
            mixed = halve(merged(mixed), bit)
        grads[1] = lax.concatenate([grads[1][0], take(grads[1][1], grad_w_out)], 0)
        grads[1] = grads[1], swap_core(grads[1])
        grads[0] = grads[0][0], take(grads[0][1])
        for p, i in ((0, 0), (0, 1), (1, 0)):
            grad_w_in = weight_grad(flat(grads[p][i]), x_rows[i], (own_half, other_half)[i], p, grad_w_in, True)
        mixed = flips(merged(mixed, grad_w_in), first, 0).reshape(tokens, width)
        grad_w_in = weight_grad(flat(take(grads[1][1])), x_rows[1], other_half, 1, grad_w_in, True)
        return (mixed, grad_w_in, grad_w_out)

    return per_device


def solution(mesh):
    placed = (P("col", "row"), P("row", "col"), P("col", "row"), P("col", "row"))
    return jax.shard_map(
        make(mesh.shape["row"], mesh.shape["col"]),
        mesh=mesh,
        in_specs=placed,
        out_specs=(P("col", "row"), P("row", "col"), P("col", "row")),
        check_vma=False,
    )
```

```python
import jax
import jax.numpy as jnp
from jax import lax
from jax.sharding import PartitionSpec as P

f32 = jnp.float32
bf16 = jnp.bfloat16


def gelu_parts(hidden):
    cdf = 0.5 * (1.0 + jax.scipy.special.erf(hidden * 0.7071067811865476))
    pdf = jnp.exp(-0.5 * hidden * hidden) * 0.3989422804014327
    return (hidden * cdf, cdf + hidden * pdf)


def add_and_split(v, got):
    rows = v.shape[0]
    total = (v.astype(f32) + got.astype(f32)).astype(bf16)
    return total[: rows // 2], total[rows // 2 :]


def weight_grad(piece, rows, half, p, into, across):
    quarter = piece.shape[1]
    at = (half * 2 + p) * quarter
    if across:
        out = jnp.dot(rows, piece, preferred_element_type=f32).astype(bf16)
        return lax.dynamic_update_slice(into, out, (0, at))
    out = lax.dot_general(piece, rows, (((0,), (0,)), ((), ())), preferred_element_type=f32).astype(bf16)
    return lax.dynamic_update_slice(into, out, (at, 0))


def make(n_row, n_col):
    row_bits = n_row.bit_length() - 1
    col_bits = n_col.bit_length() - 1
    first = tuple(range(1, row_bits))
    orders = (first, first[::-1])
    steps = len(first)

    def swap_core(v):
        return lax.ppermute(v, "row", [(i, i ^ 1) for i in range(n_row)])

    def swap_chip(v, step):
        return lax.ppermute(v, "row", [(i, i ^ (1 << orders[i & 1][step])) for i in range(n_row)])

    def part(v, axis, index):
        return lax.slice_in_dim(v, index, index + 1, axis=axis)

    def flips(v, order, axis):
        me = lax.axis_index("row")
        for k, bit in enumerate(order):
            v = jnp.where((me >> bit) & 1 == 1, jnp.flip(v, axis + k), v)
        return v

    def relative(v):
        v = v.reshape((2,) * steps + (1, v.shape[0] >> steps, v.shape[1]))
        return flips(v, first, 0)

    def turn(v):
        return v.transpose(tuple(range(steps))[::-1] + tuple(range(steps, v.ndim)))

    def after(v, *tokens):
        return lax.optimization_barrier((v,) + tokens)[0]

    def flat(v):
        return v.reshape(-1, v.shape[-1])

    def per_device(latents, w_in, w_out, cotangent):
        tokens, width = latents.shape
        cut = w_in.shape[1] // 2
        core = lax.axis_index("row") & 1
        own_half = core.astype(jnp.int32)
        other_half = 1 - own_half

        taken = []

        def take(got, *also):
            got = after(got, *taken, *also)
            taken[:] = [got]
            return got

        def ordered(v):
            plain, turned = flat(v), flat(turn(v))
            return jnp.where(core == 0, plain, turned), jnp.where(core == 0, turned, plain)

        def by_core(parts):
            own = jnp.where(core == 0, parts[0], parts[1])
            return own, swap_core(jnp.where(core == 0, parts[1], parts[0]))

        def up(x):
            return by_core(
                [
                    jnp.dot(v, w_in[:, h * cut : (h + 1) * cut], preferred_element_type=f32).astype(bf16)
                    for h, v in enumerate((flat(x), flat(turn(x))))
                ]
            )

        def back(c):
            dims = (((1,), (1,)), ((), ()))
            return by_core(
                [
                    lax.dot_general(v, w_out[h * cut : (h + 1) * cut], dims, preferred_element_type=f32).astype(bf16)
                    for h, v in enumerate((flat(c), flat(turn(c))))
                ]
            )

        def step(keep, got, k):
            keep, send = add_and_split(keep, got)
            return keep, swap_chip(send, k)

        def total(keep, got):
            return (keep.astype(f32) + got.astype(f32)).reshape((1,) * steps + (-1, tokens >> steps, cut))

        def steps_on(flight, begin, end):
            for k in range(begin, end):
                flight = step(flight[0], take(flight[1]), k)
            return flight

        def reach(v, distance):
            return lax.ppermute(v, "col", [(i, i ^ distance) for i in range(n_col)])

        x_own, c_own = relative(latents), relative(cotangent)
        near = reach(lax.concatenate([x_own, c_own], steps + 2), 1)
        x_far = [reach(x_own, d) for d in range(2, n_col)]
        x_far, near = lax.optimization_barrier((x_far, near))
        x_near = lax.concatenate([x_own, near[..., :width]], steps)
        c_near = lax.concatenate([c_own, near[..., width:]], steps)
        x_far = lax.concatenate(x_far, steps)
        x_all = lax.concatenate([x_near, x_far], steps)
        hid_near, hid_far, grad_near = up(x_near), up(x_far), back(c_near)
        x_rows = [lax.optimization_barrier(v.T) for v in ordered(x_all)]

        hid_near = step(hid_near[0], take(hid_near[1]), 0)
        hid_far = step(hid_far[0], take(hid_far[1]), 0)
        grad_near = grad_near[0], take(grad_near[1])
        c_far = [reach(after(c_own, x_far), d) for d in range(2, n_col)]
        hid_near = step(hid_near[0], take(hid_near[1], *x_rows), 1)
        grad_near = step(*grad_near, 0)
        hid_far = step(hid_far[0], take(hid_far[1]), 1)
        hid_near = steps_on(hid_near, 2, steps)
        hids = [total(hid_near[0], take(hid_near[1]))]
        c_far = lax.concatenate([take(v) for v in c_far], steps)
        grad_far = back(c_far)
        c_all = lax.concatenate([c_near, c_far], steps)
        c_rows = [lax.optimization_barrier(v) for v in ordered(c_all)]
        grad_near = step(grad_near[0], take(grad_near[1]), 1)
        hid_far = steps_on(hid_far, 2, steps)
        hids.append(total(hid_far[0], take(hid_far[1])))
        hid = lax.concatenate(hids, steps)
        act = gelu_parts(hid)[0].astype(bf16)

        def doubled(flight, k):
            return lax.concatenate([flight[0], take(flight[1])], k)

        def chips(v, begin, end):
            flight = v, swap_chip(v, end - 1)
            for k in reversed(range(begin, end - 1)):
                v = doubled(flight, k + 1)
                flight = v, swap_chip(v, k)
            return flight

        quarter = cut // 2

        def quarters(v):
            return [v[..., p * quarter : (p + 1) * quarter] for p in range(2)]

        act = chips(act, 1, steps)
        grad_far = step(grad_far[0], take(grad_far[1]), 0)
        grad_near = steps_on(grad_near, 2, steps)
        grads = [total(grad_near[0], take(grad_near[1], *c_rows))]
        grad_far = grad_far[0], take(grad_far[1])
        act = quarters(doubled(act, 1))
        grad_far = step(*grad_far, 1)
        acts = [(v, swap_chip(v, 0)) for v in act]
        grad_far = steps_on(grad_far, 2, steps)
        grads.append(total(grad_far[0], take(grad_far[1])))
        grad = lax.concatenate(grads, steps)
        hid, grad = lax.optimization_barrier((hid, grad))
        grad = chips((grad * gelu_parts(hid)[1]).astype(bf16), 1, steps)
        acts = [doubled(v, 0) for v in acts]
        acts = [(v, swap_core(v)) for v in acts]
        grad = quarters(doubled(grad, 1))
        grads = [(v, swap_chip(v, 0)) for v in grad]
        acts = [(v, take(got)) for v, got in acts]

        sums = []
        for i, half in enumerate((own_half, other_half)):
            parts = []
            for p in range(2):
                w = lax.dynamic_slice_in_dim(w_out, (half * 2 + p) * quarter, quarter, 0)
                parts.append(jnp.dot(flat(acts[p][i]), w, preferred_element_type=f32))
            sums.append((parts[0] + parts[1]).reshape(x_all.shape))
        mixed = jnp.where(core == 0, sums[0], sums[1]) + turn(jnp.where(core == 0, sums[1], sums[0]))
        mixed = mixed.astype(bf16)

        def halve(mixed, bit):
            blocks = mixed.shape[steps]
            mixed = mixed.reshape(mixed.shape[:steps] + (blocks // 2, 2) + mixed.shape[steps + 1 :])
            return (
                lax.index_in_dim(mixed, 0, steps + 1, False),
                reach(lax.index_in_dim(mixed, 1, steps + 1, False), 1 << bit),
            )

        def merged(flight, *also):
            return (flight[0].astype(f32) + take(flight[1], *also).astype(f32)).astype(bf16)

        grads[0] = lax.concatenate([grads[0][0], take(grads[0][1], mixed)], 0)
        grads[0] = grads[0], swap_core(grads[0])
        mixed = halve(mixed, 0)
        grad_w_out = jnp.zeros_like(w_out)
        for p in range(2):
            for i, half in enumerate((own_half, other_half)):
                grad_w_out = weight_grad(flat(acts[p][i]), c_rows[i], half, p, grad_w_out, False)
        grad_w_in = weight_grad(flat(grads[0][0]), x_rows[0], own_half, 0, jnp.zeros_like(w_in), True)
        for bit in range(1, col_bits):
            mixed = halve(merged(mixed), bit)
        grads[1] = lax.concatenate([grads[1][0], take(grads[1][1], grad_w_in)], 0)
        grads[1] = grads[1], swap_core(grads[1])
        grads[0] = grads[0][0], take(grads[0][1])
        for p, i in ((0, 1), (1, 0)):
            grad_w_in = weight_grad(flat(grads[p][i]), x_rows[i], (own_half, other_half)[i], p, grad_w_in, True)
        mixed = flips(merged(mixed, grad_w_in, grad_w_out), first, 0).reshape(tokens, width)
        grad_w_in = weight_grad(flat(take(grads[1][1])), x_rows[1], other_half, 1, grad_w_in, True)
        return (mixed, grad_w_in, grad_w_out)

    return per_device


def solution(mesh):
    placed = (P("col", "row"), P("row", "col"), P("col", "row"), P("col", "row"))
    return jax.shard_map(
        make(mesh.shape["row"], mesh.shape["col"]),
        mesh=mesh,
        in_specs=placed,
        out_specs=(P("col", "row"), P("row", "col"), P("col", "row")),
        check_vma=False,
    )
```

```python
import jax
import jax.numpy as jnp
from jax import lax
from jax.sharding import PartitionSpec as P

f32 = jnp.float32
bf16 = jnp.bfloat16


def gelu_parts(hidden):
    cdf = 0.5 * (1.0 + jax.scipy.special.erf(hidden * 0.7071067811865476))
    pdf = jnp.exp(-0.5 * hidden * hidden) * 0.3989422804014327
    return (hidden * cdf, cdf + hidden * pdf)


def add_and_split(v, got):
    rows = v.shape[0]
    total = (v.astype(f32) + got.astype(f32)).astype(bf16)
    return total[: rows // 2], total[rows // 2 :]


def weight_grad(piece, rows, half, p, into, across):
    quarter = piece.shape[1]
    at = (half * 2 + p) * quarter
    if across:
        out = jnp.dot(rows, piece, preferred_element_type=f32).astype(bf16)
        return lax.dynamic_update_slice(into, out, (0, at))
    out = lax.dot_general(piece, rows, (((0,), (0,)), ((), ())), preferred_element_type=f32).astype(bf16)
    return lax.dynamic_update_slice(into, out, (at, 0))


def make(n_row, n_col):
    row_bits = n_row.bit_length() - 1
    col_bits = n_col.bit_length() - 1
    first = tuple(range(1, row_bits))
    orders = (first, first[::-1])
    steps = len(first)

    def swap_core(v):
        return lax.ppermute(v, "row", [(i, i ^ 1) for i in range(n_row)])

    def swap_chip(v, step):
        return lax.ppermute(v, "row", [(i, i ^ (1 << orders[i & 1][step])) for i in range(n_row)])

    def part(v, axis, index):
        return lax.slice_in_dim(v, index, index + 1, axis=axis)

    def flips(v, order, axis):
        me = lax.axis_index("row")
        for k, bit in enumerate(order):
            v = jnp.where((me >> bit) & 1 == 1, jnp.flip(v, axis + k), v)
        return v

    def relative(v):
        v = v.reshape((2,) * steps + (1, v.shape[0] >> steps, v.shape[1]))
        return flips(v, first, 0)

    def turn(v):
        return v.transpose(tuple(range(steps))[::-1] + tuple(range(steps, v.ndim)))

    def after(v, *tokens):
        return lax.optimization_barrier((v,) + tokens)[0]

    def flat(v):
        return v.reshape(-1, v.shape[-1])

    def per_device(latents, w_in, w_out, cotangent):
        tokens, width = latents.shape
        cut = w_in.shape[1] // 2
        core = lax.axis_index("row") & 1
        own_half = core.astype(jnp.int32)
        other_half = 1 - own_half

        taken = []

        def take(got, *also):
            got = after(got, *taken, *also)
            taken[:] = [got]
            return got

        def ordered(v):
            plain, turned = flat(v), flat(turn(v))
            return jnp.where(core == 0, plain, turned), jnp.where(core == 0, turned, plain)

        def by_core(parts):
            own = jnp.where(core == 0, parts[0], parts[1])
            return own, swap_core(jnp.where(core == 0, parts[1], parts[0]))

        def up(x):
            return by_core(
                [
                    jnp.dot(v, w_in[:, h * cut : (h + 1) * cut], preferred_element_type=f32).astype(bf16)
                    for h, v in enumerate((flat(x), flat(turn(x))))
                ]
            )

        def back(c):
            dims = (((1,), (1,)), ((), ()))
            return by_core(
                [
                    lax.dot_general(v, w_out[h * cut : (h + 1) * cut], dims, preferred_element_type=f32).astype(bf16)
                    for h, v in enumerate((flat(c), flat(turn(c))))
                ]
            )

        def step(keep, got, k):
            keep, send = add_and_split(keep, got)
            return keep, swap_chip(send, k)

        def total(keep, got):
            return (keep.astype(f32) + got.astype(f32)).reshape((1,) * steps + (-1, tokens >> steps, cut))

        def steps_on(flight, begin, end):
            for k in range(begin, end):
                flight = step(flight[0], take(flight[1]), k)
            return flight

        def reach(v, distance):
            return lax.ppermute(v, "col", [(i, i ^ distance) for i in range(n_col)])

        x_own, c_own = relative(latents), relative(cotangent)
        near = take(reach(lax.concatenate([x_own, c_own], steps + 2), 1))
        x_near = lax.concatenate([x_own, near[..., :width]], steps)
        c_near = lax.concatenate([c_own, near[..., width:]], steps)
        hid_near, grad_near = up(x_near), back(c_near)
        hid_near = step(hid_near[0], take(hid_near[1]), 0)
        grad_near = step(grad_near[0], take(grad_near[1]), 0)
        hid_near = hid_near[0], take(hid_near[1])
        x_far = lax.concatenate([take(reach(x_own, d)) for d in range(2, n_col)], steps)
        c_far = [reach(after(c_own, x_far), d) for d in range(2, n_col)]
        grad_near = grad_near[0], take(grad_near[1])
        x_far = after(x_far, grad_near[1])
        hid_near = step(*hid_near, 1)
        grad_near = step(*grad_near, 1)
        hid_far = up(x_far)
        hid_far = step(hid_far[0], take(hid_far[1]), 0)
        hid_near = steps_on(hid_near, 2, steps)
        hids = [total(hid_near[0], take(hid_near[1]))]
        x_all = lax.concatenate([x_near, x_far], steps)
        x_rows = [lax.optimization_barrier(v.T) for v in ordered(x_all)]
        grad_near = steps_on(grad_near, 2, steps)
        grads = [total(grad_near[0], take(grad_near[1], *x_rows))]
        c_far = lax.concatenate([take(v) for v in c_far], steps)
        hid_far = steps_on(hid_far, 1, steps)
        hid_far = hid_far[0], take(hid_far[1])
        hids.append(total(*hid_far))
        c_far = after(c_far, hid_far[1])
        c_all = lax.concatenate([c_near, c_far], steps)
        c_rows = [lax.optimization_barrier(v) for v in ordered(c_all)]
        grad_far = back(c_far)
        hid = lax.concatenate(hids, steps)
        act = gelu_parts(hid)[0].astype(bf16)

        def doubled(flight, k):
            return lax.concatenate([flight[0], take(flight[1])], k)

        def chips(v, begin, end):
            flight = v, swap_chip(v, end - 1)
            for k in reversed(range(begin, end - 1)):
                v = doubled(flight, k + 1)
                flight = v, swap_chip(v, k)
            return flight

        quarter = cut // 2

        def quarters(v):
            return [v[..., p * quarter : (p + 1) * quarter] for p in range(2)]

        act = chips(act, 1, steps)
        grad_far = step(grad_far[0], take(grad_far[1]), 0)
        grad_far = grad_far[0], take(grad_far[1], *c_rows)
        act = quarters(doubled(act, 1))
        grad_far = step(*grad_far, 1)
        acts = [(v, swap_chip(v, 0)) for v in act]
        grad_far = steps_on(grad_far, 2, steps)
        grads.append(total(grad_far[0], take(grad_far[1])))
        grad = lax.concatenate(grads, steps)
        hid, grad = lax.optimization_barrier((hid, grad))
        grad = chips((grad * gelu_parts(hid)[1]).astype(bf16), 1, steps)
        acts = [doubled(v, 0) for v in acts]
        acts = [(v, swap_core(v)) for v in acts]
        grad_w_out = jnp.zeros_like(w_out)
        for p in range(2):
            grad_w_out = weight_grad(flat(acts[p][0]), c_rows[0], own_half, p, grad_w_out, False)
        grad = grad[0], take(grad[1], grad_w_out)
        grad = quarters(lax.concatenate(grad, 1))
        grads = [(v, swap_chip(v, 0)) for v in grad]
        acts = [(v, take(got)) for v, got in acts]

        sums = []
        for i, half in enumerate((own_half, other_half)):
            parts = []
            for p in range(2):
                w = lax.dynamic_slice_in_dim(w_out, (half * 2 + p) * quarter, quarter, 0)
                parts.append(jnp.dot(flat(acts[p][i]), w, preferred_element_type=f32))
            sums.append((parts[0] + parts[1]).reshape(x_all.shape))
        mixed = jnp.where(core == 0, sums[0], sums[1]) + turn(jnp.where(core == 0, sums[1], sums[0]))
        mixed = mixed.astype(bf16)

        def halve(mixed, bit):
            blocks = mixed.shape[steps]
            mixed = mixed.reshape(mixed.shape[:steps] + (blocks // 2, 2) + mixed.shape[steps + 1 :])
            return (
                lax.index_in_dim(mixed, 0, steps + 1, False),
                reach(lax.index_in_dim(mixed, 1, steps + 1, False), 1 << bit),
            )

        def merged(flight, *also):
            return (flight[0].astype(f32) + take(flight[1], *also).astype(f32)).astype(bf16)

        for p in range(2):
            grad_w_out = weight_grad(flat(acts[p][1]), c_rows[1], other_half, p, grad_w_out, False)
        grads[0] = grads[0][0], take(grads[0][1], mixed, grad_w_out)
        mixed = halve(mixed, 0)
        mixed = merged(mixed)
        grads[0] = lax.concatenate([grads[0][0], after(grads[0][1], mixed)], 0)
        grads[0] = grads[0], swap_core(grads[0])
        grad_w_in = weight_grad(flat(grads[0][0]), x_rows[0], own_half, 0, jnp.zeros_like(w_in), True)
        for bit in range(1, col_bits):
            mixed = halve(mixed if bit == 1 else merged(mixed), bit)
        grads[1] = lax.concatenate([grads[1][0], take(grads[1][1], grad_w_in)], 0)
        grads[1] = grads[1], swap_core(grads[1])
        grads[0] = grads[0][0], take(grads[0][1])
        for p, i in ((0, 1), (1, 0)):
            grad_w_in = weight_grad(flat(grads[p][i]), x_rows[i], (own_half, other_half)[i], p, grad_w_in, True)
        grad_w_in = weight_grad(flat(take(grads[1][1])), x_rows[1], other_half, 1, grad_w_in, True)
        mixed = merged(mixed, grad_w_in) if col_bits > 1 else mixed
        mixed = flips(mixed, first, 0).reshape(tokens, width)
        return (mixed, grad_w_in, grad_w_out)

    return per_device


def solution(mesh):
    placed = (P("col", "row"), P("row", "col"), P("col", "row"), P("col", "row"))
    return jax.shard_map(
        make(mesh.shape["row"], mesh.shape["col"]),
        mesh=mesh,
        in_specs=placed,
        out_specs=(P("col", "row"), P("row", "col"), P("col", "row")),
        check_vma=False,
    )
```

```python
import jax
import jax.numpy as jnp
from jax import lax
from jax.sharding import PartitionSpec as P

f32 = jnp.float32
bf16 = jnp.bfloat16


def gelu_parts(hidden):
    cdf = 0.5 * (1.0 + jax.scipy.special.erf(hidden * 0.7071067811865476))
    pdf = jnp.exp(-0.5 * hidden * hidden) * 0.3989422804014327
    return (hidden * cdf, cdf + hidden * pdf)


def add_and_split(v, got):
    rows = v.shape[0]
    total = (v.astype(f32) + got.astype(f32)).astype(bf16)
    return total[: rows // 2], total[rows // 2 :]


def weight_grad(piece, rows, half, p, into, across):
    quarter = piece.shape[1]
    at = (half * 2 + p) * quarter
    if across:
        out = jnp.dot(rows, piece, preferred_element_type=f32).astype(bf16)
        return lax.dynamic_update_slice(into, out, (0, at))
    out = lax.dot_general(piece, rows, (((0,), (0,)), ((), ())), preferred_element_type=f32).astype(bf16)
    return lax.dynamic_update_slice(into, out, (at, 0))


def make(n_row, n_col):
    row_bits = n_row.bit_length() - 1
    col_bits = n_col.bit_length() - 1
    first = tuple(range(1, row_bits))
    orders = (first, first[::-1])
    steps = len(first)

    def swap_core(v):
        return lax.ppermute(v, "row", [(i, i ^ 1) for i in range(n_row)])

    def swap_chip(v, step):
        return lax.ppermute(v, "row", [(i, i ^ (1 << orders[i & 1][step])) for i in range(n_row)])

    def part(v, axis, index):
        return lax.slice_in_dim(v, index, index + 1, axis=axis)

    def flips(v, order, axis):
        me = lax.axis_index("row")
        for k, bit in enumerate(order):
            v = jnp.where((me >> bit) & 1 == 1, jnp.flip(v, axis + k), v)
        return v

    def relative(v):
        v = v.reshape((2,) * steps + (1, v.shape[0] >> steps, v.shape[1]))
        return flips(v, first, 0)

    def turn(v):
        return v.transpose(tuple(range(steps))[::-1] + tuple(range(steps, v.ndim)))

    def after(v, *tokens):
        return lax.optimization_barrier((v,) + tokens)[0]

    def flat(v):
        return v.reshape(-1, v.shape[-1])

    def per_device(latents, w_in, w_out, cotangent):
        tokens, width = latents.shape
        cut = w_in.shape[1] // 2
        core = lax.axis_index("row") & 1
        own_half = core.astype(jnp.int32)
        other_half = 1 - own_half

        taken = []

        def take(got, *also):
            got = after(got, *taken, *also)
            taken[:] = [got]
            return got

        def ordered(v):
            plain, turned = flat(v), flat(turn(v))
            return jnp.where(core == 0, plain, turned), jnp.where(core == 0, turned, plain)

        def by_core(parts):
            own = jnp.where(core == 0, parts[0], parts[1])
            return own, swap_core(jnp.where(core == 0, parts[1], parts[0]))

        def up(x):
            return by_core(
                [
                    jnp.dot(v, w_in[:, h * cut : (h + 1) * cut], preferred_element_type=f32).astype(bf16)
                    for h, v in enumerate((flat(x), flat(turn(x))))
                ]
            )

        def back(c):
            dims = (((1,), (1,)), ((), ()))
            return by_core(
                [
                    lax.dot_general(v, w_out[h * cut : (h + 1) * cut], dims, preferred_element_type=f32).astype(bf16)
                    for h, v in enumerate((flat(c), flat(turn(c))))
                ]
            )

        def step(keep, got, k):
            keep, send = add_and_split(keep, got)
            return keep, swap_chip(send, k)

        def total(keep, got):
            return (keep.astype(f32) + got.astype(f32)).reshape((1,) * steps + (-1, tokens >> steps, cut))

        def steps_on(flight, begin, end):
            for k in range(begin, end):
                flight = step(flight[0], take(flight[1]), k)
            return flight

        def reach(v, distance):
            return lax.ppermute(v, "col", [(i, i ^ distance) for i in range(n_col)])

        x_own, c_own = relative(latents), relative(cotangent)
        x_far = [reach(x_own, d) for d in range(2, n_col)]
        near = reach(lax.concatenate([x_own, c_own], steps + 2), 1)
        x_far, near = lax.optimization_barrier((x_far, near))
        x_near = lax.concatenate([x_own, near[..., :width]], steps)
        c_near = lax.concatenate([c_own, near[..., width:]], steps)
        x_far = lax.concatenate(x_far, steps)
        hid_near, grad_near = up(x_near), back(c_near)
        hid_near = step(hid_near[0], take(hid_near[1]), 0)
        grad_near = grad_near[0], take(grad_near[1])
        x_far = after(x_far, grad_near[1])
        grad_near = step(*grad_near, 0)
        hid_far = up(x_far)
        c_far = [reach(after(c_own, near), d) for d in range(2, n_col)]
        x_all = lax.concatenate([x_near, x_far], steps)
        x_rows = [lax.optimization_barrier(v.T) for v in ordered(x_all)]
        hid_far = hid_far[0], take(hid_far[1])
        hid_near = hid_near[0], take(hid_near[1])
        hid_far = step(*hid_far, 0)
        hid_near = step(*hid_near, 1)
        grad_near = step(grad_near[0], take(grad_near[1], *x_rows), 1)
        hid_near = steps_on(hid_near, 2, steps)
        hids = [total(hid_near[0], take(hid_near[1]))]
        c_far = lax.concatenate([take(v) for v in c_far], steps)
        c_all = lax.concatenate([c_near, c_far], steps)
        c_rows = [lax.optimization_barrier(v) for v in ordered(c_all)]
        grad_far = back(c_far)
        hid_far = steps_on(hid_far, 1, steps)
        grad_near = steps_on(grad_near, 2, steps)
        grads = [total(grad_near[0], take(grad_near[1]))]
        hids.append(total(hid_far[0], take(hid_far[1])))
        hid = lax.concatenate(hids, steps)
        act = gelu_parts(hid)[0].astype(bf16)

        def doubled(flight, k):
            return lax.concatenate([flight[0], take(flight[1])], k)

        def chips(v, begin, end):
            flight = v, swap_chip(v, end - 1)
            for k in reversed(range(begin, end - 1)):
                v = doubled(flight, k + 1)
                flight = v, swap_chip(v, k)
            return flight

        quarter = cut // 2

        def quarters(v):
            return [v[..., p * quarter : (p + 1) * quarter] for p in range(2)]

        act = chips(act, 1, steps)
        grad_far = step(grad_far[0], take(grad_far[1]), 0)
        grad_far = grad_far[0], take(grad_far[1], *c_rows)
        act = quarters(doubled(act, 1))
        grad_far = step(*grad_far, 1)
        acts = [(v, swap_chip(v, 0)) for v in act]
        grad_far = steps_on(grad_far, 2, steps)
        grads.append(total(grad_far[0], take(grad_far[1])))
        grad = lax.concatenate(grads, steps)
        hid, grad = lax.optimization_barrier((hid, grad))
        grad = chips((grad * gelu_parts(hid)[1]).astype(bf16), 1, steps)
        def down(v, half, p):
            w = lax.dynamic_slice_in_dim(w_out, (half * 2 + p) * quarter, quarter, 0)
            return jnp.dot(flat(v), w, preferred_element_type=f32)

        own = doubled(acts[0], 0)
        got = [swap_core(own)]
        sums = [down(own, own_half, 0)]
        grad_w_out = weight_grad(flat(own), c_rows[0], own_half, 0, jnp.zeros_like(w_out), False)
        own = lax.concatenate([acts[1][0], take(acts[1][1], sums[0], grad_w_out)], 0)
        got.append(swap_core(own))
        grad = quarters(doubled(grad, 1))
        grads = [(v, swap_chip(v, 0)) for v in grad]
        got = [take(v) for v in got]
        sums.append(down(got[0], other_half, 0))
        sums[0] = (sums[0] + down(own, own_half, 1)).reshape(x_all.shape)
        sums[1] = (sums[1] + down(got[1], other_half, 1)).reshape(x_all.shape)
        mixed = jnp.where(core == 0, sums[0], sums[1]) + turn(jnp.where(core == 0, sums[1], sums[0]))
        mixed = mixed.astype(bf16)

        def halve(mixed, bit):
            blocks = mixed.shape[steps]
            mixed = mixed.reshape(mixed.shape[:steps] + (blocks // 2, 2) + mixed.shape[steps + 1 :])
            return (
                lax.index_in_dim(mixed, 0, steps + 1, False),
                reach(lax.index_in_dim(mixed, 1, steps + 1, False), 1 << bit),
            )

        def merged(flight, *also):
            return (flight[0].astype(f32) + take(flight[1], *also).astype(f32)).astype(bf16)

        for half, rows, v, p in (
            (other_half, c_rows[1], got[0], 0),
            (own_half, c_rows[0], own, 1),
            (other_half, c_rows[1], got[1], 1),
        ):
            grad_w_out = weight_grad(flat(v), rows, half, p, grad_w_out, False)
        grads[0] = grads[0][0], take(grads[0][1], mixed, grad_w_out)
        mixed = halve(mixed, 0)
        mixed = merged(mixed)
        grads[0] = lax.concatenate([grads[0][0], after(grads[0][1], mixed)], 0)
        grads[0] = grads[0], swap_core(grads[0])
        grad_w_in = weight_grad(flat(grads[0][0]), x_rows[0], own_half, 0, jnp.zeros_like(w_in), True)
        for bit in range(1, col_bits):
            mixed = halve(mixed if bit == 1 else merged(mixed), bit)
        grads[1] = lax.concatenate([grads[1][0], take(grads[1][1], grad_w_in)], 0)
        grads[1] = grads[1], swap_core(grads[1])
        grads[0] = grads[0][0], take(grads[0][1])
        for p, i in ((0, 1), (1, 0)):
            grad_w_in = weight_grad(flat(grads[p][i]), x_rows[i], (own_half, other_half)[i], p, grad_w_in, True)
        grad_w_in = weight_grad(flat(take(grads[1][1])), x_rows[1], other_half, 1, grad_w_in, True)
        mixed = merged(mixed, grad_w_in) if col_bits > 1 else mixed
        mixed = flips(mixed, first, 0).reshape(tokens, width)
        return (mixed, grad_w_in, grad_w_out)

    return per_device


def solution(mesh):
    placed = (P("col", "row"), P("row", "col"), P("col", "row"), P("col", "row"))
    return jax.shard_map(
        make(mesh.shape["row"], mesh.shape["col"]),
        mesh=mesh,
        in_specs=placed,
        out_specs=(P("col", "row"), P("row", "col"), P("col", "row")),
        check_vma=False,
    )
```

```python
import jax
import jax.numpy as jnp
from jax import lax
from jax.sharding import PartitionSpec as P

f32 = jnp.float32
bf16 = jnp.bfloat16


def gelu_parts(hidden):
    cdf = 0.5 * (1.0 + jax.scipy.special.erf(hidden * 0.7071067811865476))
    pdf = jnp.exp(-0.5 * hidden * hidden) * 0.3989422804014327
    return (hidden * cdf, cdf + hidden * pdf)


def add_and_split(v, got):
    rows = v.shape[0]
    total = (v.astype(f32) + got.astype(f32)).astype(bf16)
    return total[: rows // 2], total[rows // 2 :]


def weight_grad(piece, rows, half, p, into, across):
    quarter = piece.shape[1]
    at = (half * 2 + p) * quarter
    if across:
        out = jnp.dot(rows, piece, preferred_element_type=f32).astype(bf16)
        return lax.dynamic_update_slice(into, out, (0, at))
    out = lax.dot_general(piece, rows, (((0,), (0,)), ((), ())), preferred_element_type=f32).astype(bf16)
    return lax.dynamic_update_slice(into, out, (at, 0))


def make(n_row, n_col):
    row_bits = n_row.bit_length() - 1
    col_bits = n_col.bit_length() - 1
    first = tuple(range(1, row_bits))
    orders = (first, first[::-1])
    steps = len(first)

    def swap_core(v):
        return lax.ppermute(v, "row", [(i, i ^ 1) for i in range(n_row)])

    def swap_chip(v, step):
        return lax.ppermute(v, "row", [(i, i ^ (1 << orders[i & 1][step])) for i in range(n_row)])

    def part(v, axis, index):
        return lax.slice_in_dim(v, index, index + 1, axis=axis)

    def flips(v, order, axis):
        me = lax.axis_index("row")
        for k, bit in enumerate(order):
            v = jnp.where((me >> bit) & 1 == 1, jnp.flip(v, axis + k), v)
        return v

    def relative(v):
        v = v.reshape((2,) * steps + (1, v.shape[0] >> steps, v.shape[1]))
        return flips(v, first, 0)

    def turn(v):
        return v.transpose(tuple(range(steps))[::-1] + tuple(range(steps, v.ndim)))

    def after(v, *tokens):
        return lax.optimization_barrier((v,) + tokens)[0]

    def flat(v):
        return v.reshape(-1, v.shape[-1])

    def per_device(latents, w_in, w_out, cotangent):
        tokens, width = latents.shape
        cut = w_in.shape[1] // 2
        core = lax.axis_index("row") & 1
        own_half = core.astype(jnp.int32)
        other_half = 1 - own_half

        taken = []

        def take(got, *also):
            got = after(got, *taken, *also)
            taken[:] = [got]
            return got

        def ordered(v):
            plain, turned = flat(v), flat(turn(v))
            return jnp.where(core == 0, plain, turned), jnp.where(core == 0, turned, plain)

        def by_core(parts):
            own = jnp.where(core == 0, parts[0], parts[1])
            return own, swap_core(jnp.where(core == 0, parts[1], parts[0]))

        def up(x):
            return by_core(
                [
                    jnp.dot(v, w_in[:, h * cut : (h + 1) * cut], preferred_element_type=f32).astype(bf16)
                    for h, v in enumerate((flat(x), flat(turn(x))))
                ]
            )

        def back(c):
            dims = (((1,), (1,)), ((), ()))
            return by_core(
                [
                    lax.dot_general(v, w_out[h * cut : (h + 1) * cut], dims, preferred_element_type=f32).astype(bf16)
                    for h, v in enumerate((flat(c), flat(turn(c))))
                ]
            )

        def step(keep, got, k):
            keep, send = add_and_split(keep, got)
            return keep, swap_chip(send, k)

        def total(keep, got):
            return (keep.astype(f32) + got.astype(f32)).reshape((1,) * steps + (-1, tokens >> steps, cut))

        def steps_on(flight, begin, end):
            for k in range(begin, end):
                flight = step(flight[0], take(flight[1]), k)
            return flight

        def reach(v, distance):
            return lax.ppermute(v, "col", [(i, i ^ distance) for i in range(n_col)])

        x_own, c_own = relative(latents), relative(cotangent)
        near = take(reach(lax.concatenate([x_own, c_own], steps + 2), 1))
        x_near = lax.concatenate([x_own, near[..., :width]], steps)
        c_near = lax.concatenate([c_own, near[..., width:]], steps)
        hid_near, grad_near = up(x_near), back(c_near)
        hid_near = step(hid_near[0], take(hid_near[1]), 0)
        grad_near = step(grad_near[0], take(grad_near[1]), 0)
        hid_near = hid_near[0], take(hid_near[1])
        x_far = lax.concatenate([take(reach(x_own, d)) for d in range(2, n_col)], steps)
        c_far = [reach(after(c_own, x_far), d) for d in range(2, n_col)]
        grad_near = grad_near[0], take(grad_near[1])
        x_far = after(x_far, grad_near[1])
        hid_near = step(*hid_near, 1)
        grad_near = step(*grad_near, 1)
        hid_far = up(x_far)
        hid_far = step(hid_far[0], take(hid_far[1]), 0)
        hid_near = steps_on(hid_near, 2, steps)
        hids = [total(hid_near[0], take(hid_near[1]))]
        x_all = lax.concatenate([x_near, x_far], steps)
        x_rows = [lax.optimization_barrier(v.T) for v in ordered(x_all)]
        grad_near = steps_on(grad_near, 2, steps)
        grads = [total(grad_near[0], take(grad_near[1], *x_rows))]
        c_far = lax.concatenate([take(v) for v in c_far], steps)
        hid_far = hid_far[0], take(hid_far[1])
        c_far = after(c_far, hid_far[1])
        c_all = lax.concatenate([c_near, c_far], steps)
        c_rows = [lax.optimization_barrier(v) for v in ordered(c_all)]
        grad_far = back(c_far)
        hid_far = step(*hid_far, 1)
        hid_far = steps_on(hid_far, 2, steps)
        hids.append(total(hid_far[0], take(hid_far[1])))
        hid = lax.concatenate(hids, steps)
        act = gelu_parts(hid)[0].astype(bf16)

        def doubled(flight, k):
            return lax.concatenate([flight[0], take(flight[1])], k)

        def chips(v, begin, end):
            flight = v, swap_chip(v, end - 1)
            for k in reversed(range(begin, end - 1)):
                v = doubled(flight, k + 1)
                flight = v, swap_chip(v, k)
            return flight

        quarter = cut // 2

        def quarters(v):
            return [v[..., p * quarter : (p + 1) * quarter] for p in range(2)]

        act = chips(act, 1, steps)
        grad_far = step(grad_far[0], take(grad_far[1]), 0)
        grad_far = grad_far[0], take(grad_far[1], *c_rows)
        act = quarters(doubled(act, 1))
        grad_far = step(*grad_far, 1)
        acts = [(v, swap_chip(v, 0)) for v in act]
        grad_far = steps_on(grad_far, 2, steps)
        grads.append(total(grad_far[0], take(grad_far[1])))
        grad = lax.concatenate(grads, steps)
        hid, grad = lax.optimization_barrier((hid, grad))
        grad = chips((grad * gelu_parts(hid)[1]).astype(bf16), 1, steps)
        def down(v, half, p):
            w = lax.dynamic_slice_in_dim(w_out, (half * 2 + p) * quarter, quarter, 0)
            return jnp.dot(flat(v), w, preferred_element_type=f32)

        own = [doubled(acts[0], 0)]
        got = [swap_core(own[0])]
        grad_w_out = weight_grad(flat(own[0]), c_rows[0], own_half, 0, jnp.zeros_like(w_out), False)
        grad = quarters(lax.concatenate([grad[0], take(grad[1], grad_w_out)], 1))
        grads = [(v, swap_chip(v, 0)) for v in grad]
        own.append(doubled(acts[1], 0))
        got.append(swap_core(own[1]))
        got = [take(v) for v in got]
        sums = [
            (down(v[0], half, 0) + down(v[1], half, 1)).reshape(x_all.shape)
            for v, half in ((own, own_half), (got, other_half))
        ]
        mixed = jnp.where(core == 0, sums[0], sums[1]) + turn(jnp.where(core == 0, sums[1], sums[0]))
        mixed = mixed.astype(bf16)

        def halve(mixed, bit):
            blocks = mixed.shape[steps]
            mixed = mixed.reshape(mixed.shape[:steps] + (blocks // 2, 2) + mixed.shape[steps + 1 :])
            return (
                lax.index_in_dim(mixed, 0, steps + 1, False),
                reach(lax.index_in_dim(mixed, 1, steps + 1, False), 1 << bit),
            )

        def merged(flight, *also):
            return (flight[0].astype(f32) + take(flight[1], *also).astype(f32)).astype(bf16)

        for half, rows, v, p in (
            (other_half, c_rows[1], got[0], 0),
            (own_half, c_rows[0], own[1], 1),
            (other_half, c_rows[1], got[1], 1),
        ):
            grad_w_out = weight_grad(flat(v), rows, half, p, grad_w_out, False)
        grads[0] = grads[0][0], take(grads[0][1], mixed, grad_w_out)
        mixed = halve(mixed, 0)
        mixed = merged(mixed)
        grads[0] = lax.concatenate([grads[0][0], after(grads[0][1], mixed)], 0)
        grads[0] = grads[0], swap_core(grads[0])
        grad_w_in = weight_grad(flat(grads[0][0]), x_rows[0], own_half, 0, jnp.zeros_like(w_in), True)
        for bit in range(1, col_bits):
            mixed = halve(mixed if bit == 1 else merged(mixed), bit)
        grads[1] = lax.concatenate([grads[1][0], take(grads[1][1], grad_w_in)], 0)
        grads[1] = grads[1], swap_core(grads[1])
        grads[0] = grads[0][0], take(grads[0][1])
        for p, i in ((0, 1), (1, 0)):
            grad_w_in = weight_grad(flat(grads[p][i]), x_rows[i], (own_half, other_half)[i], p, grad_w_in, True)
        grad_w_in = weight_grad(flat(take(grads[1][1])), x_rows[1], other_half, 1, grad_w_in, True)
        mixed = merged(mixed, grad_w_in) if col_bits > 1 else mixed
        mixed = flips(mixed, first, 0).reshape(tokens, width)
        return (mixed, grad_w_in, grad_w_out)

    return per_device


def solution(mesh):
    placed = (P("col", "row"), P("row", "col"), P("col", "row"), P("col", "row"))
    return jax.shard_map(
        make(mesh.shape["row"], mesh.shape["col"]),
        mesh=mesh,
        in_specs=placed,
        out_specs=(P("col", "row"), P("row", "col"), P("col", "row")),
        check_vma=False,
    )
```

```python
import jax
import jax.numpy as jnp
from jax import lax
from jax.sharding import PartitionSpec as P

f32 = jnp.float32
bf16 = jnp.bfloat16


def gelu_parts(hidden):
    cdf = 0.5 * (1.0 + jax.scipy.special.erf(hidden * 0.7071067811865476))
    pdf = jnp.exp(-0.5 * hidden * hidden) * 0.3989422804014327
    return (hidden * cdf, cdf + hidden * pdf)


def add_and_split(v, got):
    rows = v.shape[0]
    total = (v.astype(f32) + got.astype(f32)).astype(bf16)
    return total[: rows // 2], total[rows // 2 :]


def weight_grad(piece, rows, half, p, into, across):
    quarter = piece.shape[1]
    at = (half * 2 + p) * quarter
    if across:
        out = jnp.dot(rows, piece, preferred_element_type=f32).astype(bf16)
        return lax.dynamic_update_slice(into, out, (0, at))
    out = lax.dot_general(piece, rows, (((0,), (0,)), ((), ())), preferred_element_type=f32).astype(bf16)
    return lax.dynamic_update_slice(into, out, (at, 0))


def make(n_row, n_col):
    row_bits = n_row.bit_length() - 1
    col_bits = n_col.bit_length() - 1
    first = tuple(range(1, row_bits))
    orders = (first, first[::-1])
    steps = len(first)

    def swap_core(v):
        return lax.ppermute(v, "row", [(i, i ^ 1) for i in range(n_row)])

    def swap_chip(v, step):
        return lax.ppermute(v, "row", [(i, i ^ (1 << orders[i & 1][step])) for i in range(n_row)])

    def part(v, axis, index):
        return lax.slice_in_dim(v, index, index + 1, axis=axis)

    def flips(v, order, axis):
        me = lax.axis_index("row")
        for k, bit in enumerate(order):
            v = jnp.where((me >> bit) & 1 == 1, jnp.flip(v, axis + k), v)
        return v

    def relative(v):
        v = v.reshape((2,) * steps + (1, v.shape[0] >> steps, v.shape[1]))
        return flips(v, first, 0)

    def turn(v):
        return v.transpose(tuple(range(steps))[::-1] + tuple(range(steps, v.ndim)))

    def after(v, *tokens):
        return lax.optimization_barrier((v,) + tokens)[0]

    def flat(v):
        return v.reshape(-1, v.shape[-1])

    def per_device(latents, w_in, w_out, cotangent):
        tokens, width = latents.shape
        cut = w_in.shape[1] // 2
        core = lax.axis_index("row") & 1
        own_half = core.astype(jnp.int32)
        other_half = 1 - own_half

        taken = []

        def take(got, *also):
            got = after(got, *taken, *also)
            taken[:] = [got]
            return got

        def ordered(v):
            plain, turned = flat(v), flat(turn(v))
            return jnp.where(core == 0, plain, turned), jnp.where(core == 0, turned, plain)

        def by_core(parts):
            own = jnp.where(core == 0, parts[0], parts[1])
            return own, swap_core(jnp.where(core == 0, parts[1], parts[0]))

        def up(x):
            return by_core(
                [
                    jnp.dot(v, w_in[:, h * cut : (h + 1) * cut], preferred_element_type=f32).astype(bf16)
                    for h, v in enumerate((flat(x), flat(turn(x))))
                ]
            )

        def back(c):
            dims = (((1,), (1,)), ((), ()))
            return by_core(
                [
                    lax.dot_general(v, w_out[h * cut : (h + 1) * cut], dims, preferred_element_type=f32).astype(bf16)
                    for h, v in enumerate((flat(c), flat(turn(c))))
                ]
            )

        def step(keep, got, k):
            keep, send = add_and_split(keep, got)
            return keep, swap_chip(send, k)

        def total(keep, got):
            return (keep.astype(f32) + got.astype(f32)).reshape((1,) * steps + (-1, tokens >> steps, cut))

        def steps_on(flight, begin, end):
            for k in range(begin, end):
                flight = step(flight[0], take(flight[1]), k)
            return flight

        def reach(v, distance):
            return lax.ppermute(v, "col", [(i, i ^ distance) for i in range(n_col)])

        x_own, c_own = relative(latents), relative(cotangent)
        near = take(reach(lax.concatenate([x_own, c_own], steps + 2), 1))
        x_near = lax.concatenate([x_own, near[..., :width]], steps)
        c_near = lax.concatenate([c_own, near[..., width:]], steps)
        hid_near, grad_near = up(x_near), back(c_near)
        hid_near = step(hid_near[0], take(hid_near[1]), 0)
        grad_near = step(grad_near[0], take(grad_near[1]), 0)
        hid_near = hid_near[0], take(hid_near[1])
        x_far = lax.concatenate([take(reach(x_own, d)) for d in range(2, n_col)], steps)
        c_far = [reach(after(c_own, x_far), d) for d in range(2, n_col)]
        grad_near = grad_near[0], take(grad_near[1])
        x_far = after(x_far, grad_near[1])
        hid_near = step(*hid_near, 1)
        grad_near = step(*grad_near, 1)
        hid_far = up(x_far)
        hid_far = step(hid_far[0], take(hid_far[1]), 0)
        hid_near = steps_on(hid_near, 2, steps)
        hids = [total(hid_near[0], take(hid_near[1]))]
        x_all = lax.concatenate([x_near, x_far], steps)
        x_rows = [lax.optimization_barrier(v.T) for v in ordered(x_all)]
        grad_near = steps_on(grad_near, 2, steps)
        grads = [total(grad_near[0], take(grad_near[1], *x_rows))]
        c_far = lax.concatenate([take(v) for v in c_far], steps)
        hid_far = hid_far[0], take(hid_far[1])
        c_far = after(c_far, hid_far[1])
        c_all = lax.concatenate([c_near, c_far], steps)
        c_rows = [lax.optimization_barrier(v) for v in ordered(c_all)]
        grad_far = back(c_far)
        hid_far = step(*hid_far, 1)
        hid_far = steps_on(hid_far, 2, steps)
        hids.append(total(hid_far[0], take(hid_far[1])))
        hid = lax.concatenate(hids, steps)
        act = gelu_parts(hid)[0].astype(bf16)

        def doubled(flight, k):
            return lax.concatenate([flight[0], take(flight[1])], k)

        def chips(v, begin, end):
            flight = v, swap_chip(v, end - 1)
            for k in reversed(range(begin, end - 1)):
                v = doubled(flight, k + 1)
                flight = v, swap_chip(v, k)
            return flight

        quarter = cut // 2

        def quarters(v):
            return [v[..., p * quarter : (p + 1) * quarter] for p in range(2)]

        act = chips(act, 1, steps)
        grad_far = step(grad_far[0], take(grad_far[1]), 0)
        grad_far = grad_far[0], take(grad_far[1], *c_rows)
        act = quarters(doubled(act, 1))
        grad_far = step(*grad_far, 1)
        acts = [(v, swap_chip(v, 0)) for v in act]
        grad_far = steps_on(grad_far, 2, steps)
        grads.append(total(grad_far[0], take(grad_far[1])))
        grad = lax.concatenate(grads, steps)
        hid, grad = lax.optimization_barrier((hid, grad))
        grad = chips((grad * gelu_parts(hid)[1]).astype(bf16), 1, steps)
        def down(v, half, p):
            w = lax.dynamic_slice_in_dim(w_out, (half * 2 + p) * quarter, quarter, 0)
            return jnp.dot(flat(v), w, preferred_element_type=f32)

        own = [doubled(acts[0], 0)]
        got = [swap_core(own[0])]
        grad = quarters(doubled(grad, 1))
        grads = [(v, swap_chip(v, 0)) for v in grad]
        own.append(doubled(acts[1], 0))
        got.append(swap_core(own[1]))
        got = [take(v) for v in got]
        sums = [
            (down(v[0], half, 0) + down(v[1], half, 1)).reshape(x_all.shape)
            for v, half in ((own, own_half), (got, other_half))
        ]
        mixed = jnp.where(core == 0, sums[0], sums[1]) + turn(jnp.where(core == 0, sums[1], sums[0]))
        mixed = mixed.astype(bf16)

        def halve(mixed, bit):
            blocks = mixed.shape[steps]
            mixed = mixed.reshape(mixed.shape[:steps] + (blocks // 2, 2) + mixed.shape[steps + 1 :])
            return (
                lax.index_in_dim(mixed, 0, steps + 1, False),
                reach(lax.index_in_dim(mixed, 1, steps + 1, False), 1 << bit),
            )

        def merged(flight, *also):
            return (flight[0].astype(f32) + take(flight[1], *also).astype(f32)).astype(bf16)

        grads[0] = grads[0][0], take(grads[0][1], mixed)
        mixed = halve(mixed, 0)
        grad_w_out = jnp.zeros_like(w_out)
        own = [after(v, got[1]) for v in own]
        for p in range(2):
            for i, (half, v) in enumerate(((own_half, own), (other_half, got))):
                grad_w_out = weight_grad(flat(v[p]), c_rows[i], half, p, grad_w_out, False)
        mixed = merged(mixed, grad_w_out)
        grads[0] = lax.concatenate([grads[0][0], after(grads[0][1], mixed)], 0)
        grads[0] = grads[0], swap_core(grads[0])
        grad_w_in = weight_grad(flat(grads[0][0]), x_rows[0], own_half, 0, jnp.zeros_like(w_in), True)
        for bit in range(1, col_bits):
            mixed = halve(mixed if bit == 1 else merged(mixed), bit)
        grads[1] = lax.concatenate([grads[1][0], take(grads[1][1])], 0)
        grads[1] = grads[1], swap_core(grads[1])
        grads[0] = grads[0][0], take(grads[0][1])
        for p, i in ((0, 1), (1, 0)):
            grad_w_in = weight_grad(flat(grads[p][i]), x_rows[i], (own_half, other_half)[i], p, grad_w_in, True)
        grad_w_in = weight_grad(flat(take(grads[1][1])), x_rows[1], other_half, 1, grad_w_in, True)
        mixed = merged(mixed, grad_w_in) if col_bits > 1 else mixed
        mixed = flips(mixed, first, 0).reshape(tokens, width)
        return (mixed, grad_w_in, grad_w_out)

    return per_device


def solution(mesh):
    placed = (P("col", "row"), P("row", "col"), P("col", "row"), P("col", "row"))
    return jax.shard_map(
        make(mesh.shape["row"], mesh.shape["col"]),
        mesh=mesh,
        in_specs=placed,
        out_specs=(P("col", "row"), P("row", "col"), P("col", "row")),
        check_vma=False,
    )
```

```python
import jax
import jax.numpy as jnp
from jax import lax
from jax.sharding import PartitionSpec as P

f32 = jnp.float32
bf16 = jnp.bfloat16


def gelu_parts(hidden):
    cdf = 0.5 * (1.0 + jax.scipy.special.erf(hidden * 0.7071067811865476))
    pdf = jnp.exp(-0.5 * hidden * hidden) * 0.3989422804014327
    return (hidden * cdf, cdf + hidden * pdf)


def add_and_split(v, got):
    rows = v.shape[0]
    total = (v.astype(f32) + got.astype(f32)).astype(bf16)
    return total[: rows // 2], total[rows // 2 :]


def weight_grad(piece, rows, half, p, into, across):
    quarter = piece.shape[1]
    at = (half * 2 + p) * quarter
    if across:
        out = jnp.dot(rows, piece, preferred_element_type=f32).astype(bf16)
        return lax.dynamic_update_slice(into, out, (0, at))
    out = lax.dot_general(piece, rows, (((0,), (0,)), ((), ())), preferred_element_type=f32).astype(bf16)
    return lax.dynamic_update_slice(into, out, (at, 0))


def make(n_row, n_col):
    row_bits = n_row.bit_length() - 1
    col_bits = n_col.bit_length() - 1
    first = tuple(range(1, row_bits))
    orders = (first, first[::-1])
    steps = len(first)

    def swap_core(v):
        return lax.ppermute(v, "row", [(i, i ^ 1) for i in range(n_row)])

    def swap_chip(v, step):
        return lax.ppermute(v, "row", [(i, i ^ (1 << orders[i & 1][step])) for i in range(n_row)])

    def part(v, axis, index):
        return lax.slice_in_dim(v, index, index + 1, axis=axis)

    def flips(v, order, axis):
        me = lax.axis_index("row")
        for k, bit in enumerate(order):
            v = jnp.where((me >> bit) & 1 == 1, jnp.flip(v, axis + k), v)
        return v

    def relative(v):
        v = v.reshape((2,) * steps + (1, v.shape[0] >> steps, v.shape[1]))
        return flips(v, first, 0)

    def turn(v):
        return v.transpose(tuple(range(steps))[::-1] + tuple(range(steps, v.ndim)))

    def after(v, *tokens):
        return lax.optimization_barrier((v,) + tokens)[0]

    def flat(v):
        return v.reshape(-1, v.shape[-1])

    def per_device(latents, w_in, w_out, cotangent):
        tokens, width = latents.shape
        cut = w_in.shape[1] // 2
        core = lax.axis_index("row") & 1
        own_half = core.astype(jnp.int32)
        other_half = 1 - own_half

        taken = []

        def take(got, *also):
            got = after(got, *taken, *also)
            taken[:] = [got]
            return got

        def ordered(v):
            plain, turned = flat(v), flat(turn(v))
            return jnp.where(core == 0, plain, turned), jnp.where(core == 0, turned, plain)

        def by_core(parts):
            own = jnp.where(core == 0, parts[0], parts[1])
            return own, swap_core(jnp.where(core == 0, parts[1], parts[0]))

        def up(x):
            return by_core(
                [
                    jnp.dot(v, w_in[:, h * cut : (h + 1) * cut], preferred_element_type=f32).astype(bf16)
                    for h, v in enumerate((flat(x), flat(turn(x))))
                ]
            )

        def back(c):
            dims = (((1,), (1,)), ((), ()))
            return by_core(
                [
                    lax.dot_general(v, w_out[h * cut : (h + 1) * cut], dims, preferred_element_type=f32).astype(bf16)
                    for h, v in enumerate((flat(c), flat(turn(c))))
                ]
            )

        def step(keep, got, k):
            keep, send = add_and_split(keep, got)
            return keep, swap_chip(send, k)

        def total(keep, got):
            return (keep.astype(f32) + got.astype(f32)).reshape((1,) * steps + (-1, tokens >> steps, cut))

        def steps_on(flight, begin, end):
            for k in range(begin, end):
                flight = step(flight[0], take(flight[1]), k)
            return flight

        def reach(v, distance):
            return lax.ppermute(v, "col", [(i, i ^ distance) for i in range(n_col)])

        x_own, c_own = relative(latents), relative(cotangent)
        near = take(reach(lax.concatenate([x_own, c_own], steps + 2), 1))
        x_near = lax.concatenate([x_own, near[..., :width]], steps)
        c_near = lax.concatenate([c_own, near[..., width:]], steps)
        hid_near, grad_near = up(x_near), back(c_near)
        hid_near = step(hid_near[0], take(hid_near[1]), 0)
        grad_near = step(grad_near[0], take(grad_near[1]), 0)
        hid_near = hid_near[0], take(hid_near[1])
        x_far = lax.concatenate([take(reach(x_own, d)) for d in range(2, n_col)], steps)
        c_far = [reach(after(c_own, x_far), d) for d in range(2, n_col)]
        grad_near = grad_near[0], take(grad_near[1])
        x_far = after(x_far, grad_near[1])
        hid_near = step(*hid_near, 1)
        grad_near = step(*grad_near, 1)
        hid_far = up(x_far)
        hid_far = step(hid_far[0], take(hid_far[1]), 0)
        hid_near = steps_on(hid_near, 2, steps)
        hids = [total(hid_near[0], take(hid_near[1]))]
        x_all = lax.concatenate([x_near, x_far], steps)
        x_rows = [lax.optimization_barrier(v.T) for v in ordered(x_all)]
        grad_near = steps_on(grad_near, 2, steps)
        grads = [total(grad_near[0], take(grad_near[1], *x_rows))]
        hid_far = steps_on(hid_far, 1, steps)
        hids.append(total(hid_far[0], take(hid_far[1])))
        hid = lax.concatenate(hids, steps)
        act = gelu_parts(hid)[0].astype(bf16)
        c_far = lax.concatenate([take(v) for v in c_far], steps)
        c_all = lax.concatenate([c_near, c_far], steps)
        c_rows = [lax.optimization_barrier(v) for v in ordered(c_all)]
        grad_far = back(c_far)

        def doubled(flight, k):
            return lax.concatenate([flight[0], take(flight[1])], k)

        def chips(v, begin, end):
            flight = v, swap_chip(v, end - 1)
            for k in reversed(range(begin, end - 1)):
                v = doubled(flight, k + 1)
                flight = v, swap_chip(v, k)
            return flight

        quarter = cut // 2

        def quarters(v):
            return [v[..., p * quarter : (p + 1) * quarter] for p in range(2)]

        act = chips(act, 1, steps)
        act = quarters(doubled(act, 1))
        acts = [(v, swap_chip(v, 0)) for v in act]
        grad_far = step(grad_far[0], take(grad_far[1], *c_rows), 0)
        own = [doubled(acts[0], 0)]
        got = [swap_core(own[0])]
        grad_far = step(grad_far[0], take(grad_far[1]), 1)
        own.append(doubled(acts[1], 0))
        got.append(swap_core(own[1]))
        grad_far = steps_on(grad_far, 2, steps)
        grads.append(total(grad_far[0], take(grad_far[1])))
        grad = lax.concatenate(grads, steps)
        hid, grad = lax.optimization_barrier((hid, grad))
        grad = chips((grad * gelu_parts(hid)[1]).astype(bf16), 1, steps)
        got[0] = take(got[0])
        grad = grad[0], take(grad[1])
        late = grad[1]
        grad = quarters(lax.concatenate(grad, 1))
        grads = [(v, swap_chip(v, 0)) for v in grad]
        got[1] = take(got[1])
        def down(v, half, p):
            w = lax.dynamic_slice_in_dim(w_out, (half * 2 + p) * quarter, quarter, 0)
            return jnp.dot(flat(v), w, preferred_element_type=f32)

        sums = [
            (down(v[0], half, 0) + down(v[1], half, 1)).reshape(x_all.shape)
            for v, half in ((own, own_half), (got, other_half))
        ]
        mixed = jnp.where(core == 0, sums[0], sums[1]) + turn(jnp.where(core == 0, sums[1], sums[0]))
        mixed = mixed.astype(bf16)

        def halve(mixed, bit):
            blocks = mixed.shape[steps]
            mixed = mixed.reshape(mixed.shape[:steps] + (blocks // 2, 2) + mixed.shape[steps + 1 :])
            return (
                lax.index_in_dim(mixed, 0, steps + 1, False),
                reach(lax.index_in_dim(mixed, 1, steps + 1, False), 1 << bit),
            )

        def merged(flight, *also):
            return (flight[0].astype(f32) + take(flight[1], *also).astype(f32)).astype(bf16)

        grads[0] = grads[0][0], take(grads[0][1], mixed)
        mixed = halve(mixed, 0)
        grad_w_out = jnp.zeros_like(w_out)
        own = [after(v, late) for v in own]
        for p in range(2):
            for i, (half, v) in enumerate(((own_half, own), (other_half, got))):
                grad_w_out = weight_grad(flat(v[p]), c_rows[i], half, p, grad_w_out, False)
        mixed = merged(mixed, grad_w_out)
        grads[0] = lax.concatenate([grads[0][0], after(grads[0][1], mixed)], 0)
        grads[0] = grads[0], swap_core(grads[0])
        grad_w_in = weight_grad(flat(grads[0][0]), x_rows[0], own_half, 0, jnp.zeros_like(w_in), True)
        for bit in range(1, col_bits):
            mixed = halve(mixed if bit == 1 else merged(mixed), bit)
        grads[1] = lax.concatenate([grads[1][0], take(grads[1][1])], 0)
        grads[1] = grads[1], swap_core(grads[1])
        grads[0] = grads[0][0], take(grads[0][1])
        for p, i in ((0, 1), (1, 0)):
            grad_w_in = weight_grad(flat(grads[p][i]), x_rows[i], (own_half, other_half)[i], p, grad_w_in, True)
        grad_w_in = weight_grad(flat(take(grads[1][1])), x_rows[1], other_half, 1, grad_w_in, True)
        mixed = merged(mixed, grad_w_in) if col_bits > 1 else mixed
        mixed = flips(mixed, first, 0).reshape(tokens, width)
        return (mixed, grad_w_in, grad_w_out)

    return per_device


def solution(mesh):
    placed = (P("col", "row"), P("row", "col"), P("col", "row"), P("col", "row"))
    return jax.shard_map(
        make(mesh.shape["row"], mesh.shape["col"]),
        mesh=mesh,
        in_specs=placed,
        out_specs=(P("col", "row"), P("row", "col"), P("col", "row")),
        check_vma=False,
    )
```

```python
import jax
import jax.numpy as jnp
from jax import lax
from jax.sharding import PartitionSpec as P

f32 = jnp.float32
bf16 = jnp.bfloat16


def gelu_parts(hidden):
    cdf = 0.5 * (1.0 + jax.scipy.special.erf(hidden * 0.7071067811865476))
    pdf = jnp.exp(-0.5 * hidden * hidden) * 0.3989422804014327
    return (hidden * cdf, cdf + hidden * pdf)


def make(n_row, n_col):
    row_bits = n_row.bit_length() - 1
    col_bits = n_col.bit_length() - 1
    first = tuple(range(1, row_bits))
    orders = (first, first[::-1])
    steps = len(first)

    def swap_core(v):
        return lax.ppermute(v, "row", [(i, i ^ 1) for i in range(n_row)])

    def swap_chip(v, step):
        return lax.ppermute(v, "row", [(i, i ^ (1 << orders[i & 1][step])) for i in range(n_row)])

    def swap_col(v, bit):
        return lax.ppermute(v, "col", [(i, i ^ (1 << bit)) for i in range(n_col)])

    def part(v, axis, index):
        return lax.slice_in_dim(v, index, index + 1, axis=axis)

    def flips(v, order, axis):
        me = lax.axis_index("row")
        for k, bit in enumerate(order):
            v = jnp.where((me >> bit) & 1 == 1, jnp.flip(v, axis + k), v)
        return v

    def relative(v):
        v = v.reshape((2,) * steps + (1, v.shape[0] >> steps, v.shape[1]))
        return flips(v, first, 0)

    def turn(v):
        return v.transpose(tuple(range(steps))[::-1] + tuple(range(steps, v.ndim)))

    def after(v, *tokens):
        return lax.optimization_barrier((v,) + tokens)[0]

    def flat(v):
        return v.reshape(-1, v.shape[-1])

    def scatter(parts):
        core = lax.axis_index("row") & 1
        second = turn(parts[1])
        got = swap_core(jnp.where(core == 0, second, parts[0]))
        v = jnp.where(core == 0, parts[0], second)
        v = (v.astype(f32) + got.astype(f32)).astype(bf16)
        seen = [v]
        for k in range(steps):
            got = swap_chip(part(v, k, 1), k)
            seen.append(got)
            v = part(v, k, 0).astype(f32) + got.astype(f32)
            if k + 1 < steps:
                v = v.astype(bf16)
        return v, seen

    def gather_chips(v, stop):
        for k in reversed(range(stop, steps)):
            v = lax.concatenate([v, swap_chip(v, k)], k)
        return v

    def per_device(latents, w_in, w_out, cotangent):
        tokens, width = latents.shape
        cut = w_in.shape[1] // 2
        core = lax.axis_index("row") & 1

        def double(v, bit):
            got = swap_col(v, bit)
            return got, lax.concatenate([v, got], steps)

        halves = [slice(h * cut, (h + 1) * cut) for h in (0, 1)]

        def up(x):
            parts = [jnp.dot(flat(x), w_in[:, h], preferred_element_type=f32) for h in halves]
            return scatter([v.astype(bf16).reshape(x.shape[:-1] + (cut,)) for v in parts])

        def back(c):
            parts = [
                lax.dot_general(flat(c), w_out[h], (((1,), (1,)), ((), ())), preferred_element_type=f32)
                for h in halves
            ]
            return scatter([v.astype(bf16).reshape(c.shape[:-1] + (cut,)) for v in parts])

        _, x_all = double(relative(latents), 0)
        _, c_all = double(relative(cotangent), 0)
        hid, seen_hid = up(x_all)
        grad, seen_grad = back(c_all)
        hids, grads = [hid], [grad]
        for bit in range(1, col_bits):
            x, x_all = double(x_all, bit)
            x = after(x, seen_hid[1], seen_grad[0])
            c, c_all = double(after(c_all, x), bit)
            hid, seen_hid = up(x)
            grad, seen_grad = back(after(c, seen_grad[1], seen_hid[1]))
            hids.append(hid)
            grads.append(grad)

        hid = jnp.concatenate(hids, steps)
        act = gelu_parts(hid)[0].astype(bf16)
        grad = jnp.concatenate(grads, steps)
        hid, grad = lax.optimization_barrier((hid, grad))
        grad = (grad * gelu_parts(hid)[1]).astype(bf16)

        def gather(v):
            v = gather_chips(v, 1)
            quarter = cut // 2
            firsts, seconds = [], []
            for p in range(2):
                w = gather_chips_last(v[..., p * quarter : (p + 1) * quarter])
                got = swap_core(w)
                firsts.append(jnp.where(core == 0, w, got))
                seconds.append(turn(jnp.where(core == 0, got, w)))
            return lax.optimization_barrier(lax.concatenate(firsts + seconds, steps + 2))

        def gather_chips_last(v):
            return lax.concatenate([v, swap_chip(v, 0)], 0)

        act_all = gather(act)
        lead = act_all.shape[:-1]

        mixed = jnp.dot(flat(act_all), w_out, preferred_element_type=f32).astype(bf16).reshape(lead + (width,))

        def halve(mixed, bit):
            blocks = mixed.shape[steps]
            mixed = mixed.reshape(mixed.shape[:steps] + (blocks // 2, 2) + mixed.shape[steps + 1 :])
            return (
                lax.index_in_dim(mixed, 0, steps + 1, False),
                swap_col(lax.index_in_dim(mixed, 1, steps + 1, False), bit),
            )

        def merged(kept, got):
            return (kept.astype(f32) + got.astype(f32)).astype(bf16)

        plain, turned = flat(x_all), flat(turn(x_all))
        x_rows = [
            lax.optimization_barrier(jnp.where(core == h, plain, turned).T) for h in (0, 1)
        ]
        quarter = cut // 2

        def weight_grad(piece, rows, half, p, into):
            out = jnp.dot(rows, flat(piece), preferred_element_type=f32).astype(bf16)
            return lax.dynamic_update_slice(into, out, (0, (half * 2 + p) * quarter))

        own_half = core.astype(jnp.int32)
        other_half = 1 - own_half
        for k in reversed(range(1, steps)):
            grad = lax.concatenate([grad, after(swap_chip(grad, k), mixed)], k)
        near_got = swap_chip(grad[..., :quarter], 0)
        kept, got = halve(mixed, 0)
        grad_w_out = lax.dot_general(
            flat(act_all), flat(c_all), (((0,), (0,)), ((), ())), preferred_element_type=f32
        ).astype(bf16)
        near_got, got, grad_w_out = lax.optimization_barrier((near_got, got, grad_w_out))
        mixed = merged(kept, got)
        own = [lax.concatenate([grad[..., :quarter], near_got], 0)]
        other = [swap_core(own[0])]
        last = after(grad[..., quarter:], near_got)
        last_got = swap_chip(last, 0)
        grad_w_in = weight_grad(own[0], x_rows[0], own_half, 0, jnp.zeros_like(w_in))
        grad_w_in = weight_grad(other[0], x_rows[1], other_half, 0, grad_w_in)
        for bit in range(1, col_bits):
            kept, got = halve(mixed, bit)
            if bit + 1 < col_bits:
                mixed = merged(kept, got)
        own.append(lax.concatenate([last, after(last_got, grad_w_in)], 0))
        other.append(swap_core(own[1]))
        grad_w_in = weight_grad(own[1], x_rows[0], own_half, 1, grad_w_in)
        if col_bits > 1:
            got = after(got, grad_w_in)
            mixed = merged(kept, got)
        mixed = flips(mixed, first, 0).reshape(tokens, width)
        grad_w_in = weight_grad(after(other[1], got), x_rows[1], other_half, 1, grad_w_in)
        return (mixed, grad_w_in, grad_w_out)

    return per_device


def solution(mesh):
    placed = (P("col", "row"), P("row", "col"), P("col", "row"), P("col", "row"))
    return jax.shard_map(
        make(mesh.shape["row"], mesh.shape["col"]),
        mesh=mesh,
        in_specs=placed,
        out_specs=(P("col", "row"), P("row", "col"), P("col", "row")),
        check_vma=False,
    )
```

```python
import jax
import jax.numpy as jnp
from jax import lax
from jax.sharding import PartitionSpec as P

f32 = jnp.float32
bf16 = jnp.bfloat16


def gelu_parts(hidden):
    cdf = 0.5 * (1.0 + jax.scipy.special.erf(hidden * 0.7071067811865476))
    pdf = jnp.exp(-0.5 * hidden * hidden) * 0.3989422804014327
    return (hidden * cdf, cdf + hidden * pdf)


def make(n_row, n_col):
    row_bits = n_row.bit_length() - 1
    col_bits = n_col.bit_length() - 1
    first = tuple(range(1, row_bits))
    orders = (first, first[::-1])
    steps = len(first)

    def swap_core(v):
        return lax.ppermute(v, "row", [(i, i ^ 1) for i in range(n_row)])

    def swap_chip(v, step):
        return lax.ppermute(v, "row", [(i, i ^ (1 << orders[i & 1][step])) for i in range(n_row)])

    def swap_col(v, bit):
        return lax.ppermute(v, "col", [(i, i ^ (1 << bit)) for i in range(n_col)])

    def part(v, axis, index):
        return lax.slice_in_dim(v, index, index + 1, axis=axis)

    def flips(v, order, axis):
        me = lax.axis_index("row")
        for k, bit in enumerate(order):
            v = jnp.where((me >> bit) & 1 == 1, jnp.flip(v, axis + k), v)
        return v

    def relative(v):
        v = v.reshape((2,) * steps + (1, v.shape[0] >> steps, v.shape[1]))
        return flips(v, first, 0)

    def turn(v):
        return v.transpose(tuple(range(steps))[::-1] + tuple(range(steps, v.ndim)))

    def after(v, *tokens):
        return lax.optimization_barrier((v,) + tokens)[0]

    def flat(v):
        return v.reshape(-1, v.shape[-1])

    def scatter(parts):
        core = lax.axis_index("row") & 1
        second = turn(parts[1])
        got = swap_core(jnp.where(core == 0, second, parts[0]))
        v = jnp.where(core == 0, parts[0], second)
        v = (v.astype(f32) + got.astype(f32)).astype(bf16)
        seen = [v]
        for k in range(steps):
            got = swap_chip(part(v, k, 1), k)
            seen.append(got)
            v = part(v, k, 0).astype(f32) + got.astype(f32)
            if k + 1 < steps:
                v = v.astype(bf16)
        return v, seen

    def per_device(latents, w_in, w_out, cotangent):
        tokens, width = latents.shape
        cut = w_in.shape[1] // 2
        core = lax.axis_index("row") & 1

        def double(v, bit):
            got = swap_col(v, bit)
            return got, lax.concatenate([v, got], steps)

        halves = [slice(h * cut, (h + 1) * cut) for h in (0, 1)]

        def up(x):
            parts = [jnp.dot(flat(x), w_in[:, h], preferred_element_type=f32) for h in halves]
            return scatter([v.astype(bf16).reshape(x.shape[:-1] + (cut,)) for v in parts])

        def back(c):
            parts = [
                lax.dot_general(flat(c), w_out[h], (((1,), (1,)), ((), ())), preferred_element_type=f32)
                for h in halves
            ]
            return scatter([v.astype(bf16).reshape(c.shape[:-1] + (cut,)) for v in parts])

        _, x_all = double(relative(latents), 0)
        _, c_all = double(relative(cotangent), 0)
        hid, seen_hid = up(x_all)
        grad, seen_grad = back(c_all)
        hids, grads = [hid], [grad]
        for bit in range(1, col_bits):
            x, x_all = double(x_all, bit)
            x = after(x, seen_hid[1], seen_grad[0])
            c, c_all = double(after(c_all, x), bit)
            hid, seen_hid = up(x)
            grad, seen_grad = back(after(c, seen_grad[1], seen_hid[1]))
            hids.append(hid)
            grads.append(grad)

        hid = jnp.concatenate(hids, steps)
        act = gelu_parts(hid)[0].astype(bf16)
        grad = jnp.concatenate(grads, steps)
        hid, grad = lax.optimization_barrier((hid, grad))
        grad = (grad * gelu_parts(hid)[1]).astype(bf16)

        def gather(v, room):
            quarter = cut // 2
            firsts, seconds = [], []
            for p in range(2):
                w = v[..., p * quarter : (p + 1) * quarter]
                got = swap_chip(w, 0)
                if p == 1:
                    got, room = lax.optimization_barrier((got, room))
                w = lax.concatenate([w, got], 0)
                got = swap_core(w)
                firsts.append(jnp.where(core == 0, w, got))
                seconds.append(turn(jnp.where(core == 0, got, w)))
            return lax.optimization_barrier(lax.concatenate(firsts + seconds, steps + 2)), room

        for k in reversed(range(1, steps)):
            act = lax.concatenate([act, swap_chip(act, k)], k)
        blank = lax.slice(flat(x_all), (0, 0), (1, 1)) * 0
        grad_w_in = jnp.broadcast_to(blank, w_in.shape)
        act_all, grad_w_in = gather(act, grad_w_in)
        lead = act_all.shape[:-1]

        mixed = jnp.dot(flat(act_all), w_out, preferred_element_type=f32).astype(bf16).reshape(lead + (width,))

        def halve(mixed, bit):
            blocks = mixed.shape[steps]
            mixed = mixed.reshape(mixed.shape[:steps] + (blocks // 2, 2) + mixed.shape[steps + 1 :])
            return (
                lax.index_in_dim(mixed, 0, steps + 1, False),
                swap_col(lax.index_in_dim(mixed, 1, steps + 1, False), bit),
            )

        def merged(kept, got):
            return (kept.astype(f32) + got.astype(f32)).astype(bf16)

        plain, turned = flat(x_all), flat(turn(x_all))
        x_rows = [
            lax.optimization_barrier(jnp.where(core == h, plain, turned).T) for h in (0, 1)
        ]
        quarter = cut // 2

        def weight_grad(piece, rows, half, p, into):
            out = jnp.dot(rows, flat(piece), preferred_element_type=f32).astype(bf16)
            return lax.dynamic_update_slice(into, out, (0, (half * 2 + p) * quarter))

        own_half = core.astype(jnp.int32)
        other_half = 1 - own_half
        for k in reversed(range(1, steps)):
            grad = lax.concatenate([grad, after(swap_chip(grad, k), mixed)], k)
        near_got = swap_chip(grad[..., :quarter], 0)
        kept, got = halve(mixed, 0)
        grad_w_out = lax.dot_general(
            flat(act_all), flat(c_all), (((0,), (0,)), ((), ())), preferred_element_type=f32
        ).astype(bf16)
        near_got, got, grad_w_out = lax.optimization_barrier((near_got, got, grad_w_out))
        mixed = merged(kept, got)
        own = [lax.concatenate([grad[..., :quarter], near_got], 0)]
        other = [swap_core(own[0])]
        last = after(grad[..., quarter:], near_got)
        last_got = swap_chip(last, 0)
        grad_w_in = weight_grad(own[0], x_rows[0], own_half, 0, grad_w_in)
        grad_w_in = weight_grad(other[0], x_rows[1], other_half, 0, grad_w_in)
        for bit in range(1, col_bits):
            kept, got = halve(mixed, bit)
            if bit + 1 < col_bits:
                mixed = merged(kept, got)
        last_got, got, grad_w_in = lax.optimization_barrier((last_got, got, grad_w_in))
        own.append(lax.concatenate([last, last_got], 0))
        other.append(swap_core(own[1]))
        grad_w_in = weight_grad(own[1], x_rows[0], own_half, 1, grad_w_in)
        if col_bits > 1:
            mixed = merged(kept, got)
        mixed = flips(mixed, first, 0).reshape(tokens, width)
        grad_w_in = weight_grad(after(other[1], mixed), x_rows[1], other_half, 1, grad_w_in)
        return (mixed, grad_w_in, grad_w_out)

    return per_device


def solution(mesh):
    placed = (P("col", "row"), P("row", "col"), P("col", "row"), P("col", "row"))
    return jax.shard_map(
        make(mesh.shape["row"], mesh.shape["col"]),
        mesh=mesh,
        in_specs=placed,
        out_specs=(P("col", "row"), P("row", "col"), P("col", "row")),
        check_vma=False,
    )
```

```python
import jax
import jax.numpy as jnp
from jax import lax
from jax.sharding import PartitionSpec as P

f32 = jnp.float32
bf16 = jnp.bfloat16


def gelu_parts(hidden):
    cdf = 0.5 * (1.0 + jax.scipy.special.erf(hidden * 0.7071067811865476))
    pdf = jnp.exp(-0.5 * hidden * hidden) * 0.3989422804014327
    return (hidden * cdf, cdf + hidden * pdf)


def make(n_row, n_col):
    row_bits = n_row.bit_length() - 1
    col_bits = n_col.bit_length() - 1
    first = tuple(range(1, row_bits))
    orders = (first, first[::-1])
    steps = len(first)

    def swap_core(v):
        return lax.ppermute(v, "row", [(i, i ^ 1) for i in range(n_row)])

    def swap_chip(v, step):
        return lax.ppermute(v, "row", [(i, i ^ (1 << orders[i & 1][step])) for i in range(n_row)])

    def swap_col(v, bit):
        return lax.ppermute(v, "col", [(i, i ^ (1 << bit)) for i in range(n_col)])

    def part(v, axis, index):
        return lax.slice_in_dim(v, index, index + 1, axis=axis)

    def flips(v, order, axis):
        me = lax.axis_index("row")
        for k, bit in enumerate(order):
            v = jnp.where((me >> bit) & 1 == 1, jnp.flip(v, axis + k), v)
        return v

    def relative(v):
        v = v.reshape((2,) * steps + (1, v.shape[0] >> steps, v.shape[1]))
        return flips(v, first, 0)

    def turn(v):
        return v.transpose(tuple(range(steps))[::-1] + tuple(range(steps, v.ndim)))

    def after(v, *tokens):
        return lax.optimization_barrier((v,) + tokens)[0]

    def flat(v):
        return v.reshape(-1, v.shape[-1])

    def scatter(parts):
        core = lax.axis_index("row") & 1
        second = turn(parts[1])
        got = swap_core(jnp.where(core == 0, second, parts[0]))
        v = jnp.where(core == 0, parts[0], second)
        v = (v.astype(f32) + got.astype(f32)).astype(bf16)
        seen = [v]
        for k in range(steps):
            got = swap_chip(part(v, k, 1), k)
            seen.append(got)
            v = part(v, k, 0).astype(f32) + got.astype(f32)
            if k + 1 < steps:
                v = v.astype(bf16)
        return v, seen

    def per_device(latents, w_in, w_out, cotangent):
        tokens, width = latents.shape
        cut = w_in.shape[1] // 2
        core = lax.axis_index("row") & 1

        def double(v, bit):
            got = swap_col(v, bit)
            return got, lax.concatenate([v, got], steps)

        halves = [slice(h * cut, (h + 1) * cut) for h in (0, 1)]

        def up(x):
            parts = [jnp.dot(flat(x), w_in[:, h], preferred_element_type=f32) for h in halves]
            return scatter([v.astype(bf16).reshape(x.shape[:-1] + (cut,)) for v in parts])

        def back(c):
            parts = [
                lax.dot_general(flat(c), w_out[h], (((1,), (1,)), ((), ())), preferred_element_type=f32)
                for h in halves
            ]
            return scatter([v.astype(bf16).reshape(c.shape[:-1] + (cut,)) for v in parts])

        _, x_all = double(relative(latents), 0)
        _, c_all = double(relative(cotangent), 0)
        hid, seen_hid = up(x_all)
        grad, seen_grad = back(c_all)
        hids, grads = [hid], [grad]
        for bit in range(1, col_bits):
            x, x_all = double(x_all, bit)
            x = after(x, seen_hid[1], seen_grad[0])
            c, c_all = double(after(c_all, x), bit)
            hid, seen_hid = up(x)
            grad, seen_grad = back(after(c, seen_grad[1], seen_hid[1]))
            hids.append(hid)
            grads.append(grad)

        hid = jnp.concatenate(hids, steps)
        act = gelu_parts(hid)[0].astype(bf16)
        grad = jnp.concatenate(grads, steps)
        hid, grad = lax.optimization_barrier((hid, grad))
        grad = (grad * gelu_parts(hid)[1]).astype(bf16)

        def gather(v, room):
            quarter = cut // 2
            firsts, seconds = [], []
            for p in range(2):
                w = v[..., p * quarter : (p + 1) * quarter]
                got = swap_chip(w, 0)
                if p == 1:
                    got, room = lax.optimization_barrier((got, room))
                w = lax.concatenate([w, got], 0)
                got = swap_core(w)
                firsts.append(jnp.where(core == 0, w, got))
                seconds.append(turn(jnp.where(core == 0, got, w)))
            return lax.optimization_barrier(lax.concatenate(firsts + seconds, steps + 2)), room

        for k in reversed(range(1, steps)):
            act = lax.concatenate([act, swap_chip(act, k)], k)
        blank = lax.slice(flat(x_all), (0, 0), (1, 1)) * 0
        grad_w_in = jnp.broadcast_to(blank, w_in.shape)
        act_all, grad_w_in = gather(act, grad_w_in)
        lead = act_all.shape[:-1]

        mixed = jnp.dot(flat(act_all), w_out, preferred_element_type=f32).astype(bf16).reshape(lead + (width,))

        def halve(mixed, bit):
            blocks = mixed.shape[steps]
            mixed = mixed.reshape(mixed.shape[:steps] + (blocks // 2, 2) + mixed.shape[steps + 1 :])
            return (
                lax.index_in_dim(mixed, 0, steps + 1, False),
                swap_col(lax.index_in_dim(mixed, 1, steps + 1, False), bit),
            )

        def merged(kept, got):
            return (kept.astype(f32) + got.astype(f32)).astype(bf16)

        plain, turned = flat(x_all), flat(turn(x_all))
        x_rows = [
            lax.optimization_barrier(jnp.where(core == h, plain, turned).T) for h in (0, 1)
        ]
        quarter = cut // 2

        def weight_grad(piece, rows, half, p, into):
            out = jnp.dot(rows, flat(piece), preferred_element_type=f32).astype(bf16)
            return lax.dynamic_update_slice(into, out, (0, (half * 2 + p) * quarter))

        own_half = core.astype(jnp.int32)
        other_half = 1 - own_half
        for k in reversed(range(1, steps)):
            grad = lax.concatenate([grad, after(swap_chip(grad, k), mixed)], k)
        near_got = swap_chip(grad[..., :quarter], 0)
        kept, got = halve(mixed, 0)
        grad_w_out = lax.dot_general(
            flat(act_all), flat(c_all), (((0,), (0,)), ((), ())), preferred_element_type=f32
        ).astype(bf16)
        near_got, got, grad_w_out = lax.optimization_barrier((near_got, got, grad_w_out))
        mixed = merged(kept, got)
        own = [lax.concatenate([grad[..., :quarter], near_got], 0)]
        other = [swap_core(own[0])]
        last = after(grad[..., quarter:], near_got)
        last_got = swap_chip(last, 0)
        grad_w_in = weight_grad(own[0], x_rows[0], own_half, 0, grad_w_in)
        for bit in range(1, col_bits):
            kept, got = halve(mixed, bit)
            if bit + 1 < col_bits:
                mixed = merged(kept, got)
        last_got, got, grad_w_in = lax.optimization_barrier((last_got, got, grad_w_in))
        own.append(lax.concatenate([last, last_got], 0))
        other.append(swap_core(own[1]))
        grad_w_in = weight_grad(other[0], x_rows[1], other_half, 0, grad_w_in)
        grad_w_in = weight_grad(own[1], x_rows[0], own_half, 1, grad_w_in)
        if col_bits > 1:
            mixed = merged(kept, got)
        mixed = flips(mixed, first, 0).reshape(tokens, width)
        grad_w_in = weight_grad(after(other[1], mixed), x_rows[1], other_half, 1, grad_w_in)
        return (mixed, grad_w_in, grad_w_out)

    return per_device


def solution(mesh):
    placed = (P("col", "row"), P("row", "col"), P("col", "row"), P("col", "row"))
    return jax.shard_map(
        make(mesh.shape["row"], mesh.shape["col"]),
        mesh=mesh,
        in_specs=placed,
        out_specs=(P("col", "row"), P("row", "col"), P("col", "row")),
        check_vma=False,
    )
```
